32 devices in a mesh: dp: 4 (over x, core), sector: 8 (over z, y).
Axes of the slice: x: 2, y: 2, z: 4, core: 2. Of those that a mesh axis runs over, the one named last changes fastest.
Arguments:
- hits: bfloat16 [4, 16384, 256], P('dp', 'sector'), may hold values from -6 to 6
- tiles: bfloat16 [4, 128, 8, 128, 128], P('dp', 'sector'), may hold values from -0.1875 to 0.1875
- sources: int32 [4, 128, 8], P('dp', 'sector'), may hold values from 0 to 23
- send_list: int32 [4, 8, 2, 4], P('dp'), may hold values from 0 to 15, as said below
- w_message: bfloat16 [2, 256, 256], replicated, may hold values from -0.375 to 0.375
- w_self: bfloat16 [2, 256, 256], replicated, may hold values from -0.375 to 0.375
- cotangent: float32 [4, 16384, 256], P('dp', 'sector'), may hold values from -6 to 6
Outputs:
- hit_output: bfloat16 [4, 16384, 256], P('dp', 'sector')
- hit_grad: float32 [4, 16384, 256], P('dp', 'sector')
- message_grad: float32 [2, 256, 256], replicated
- self_grad: float32 [2, 256, 256], replicated
The draws below stay inside these ranges and needn't reach their ends.
Inputs may be any that keep to these rules, and one draw needn't show every extreme that they name: `send_list`: each list holds 4 distinct local block numbers of its sector.
All inputs are finite; a program needn't handle non-finite values.
Results may differ from the reference program's by a relative error of at most 0.007.
Values may be sent and summed in bfloat16 or wider, within the bound.
A program may use at most 128 MiB of HBM per device.

```python
import jax
import jax.numpy as jnp
from jax import lax

F = 256
TILE = 128
K = 8
S = 4
LAYERS = 2
HB = 16
EVENTS = 4
SECTORS = 8
BLOCKS = 128
ROWS = 16384


def draw_send_list(key, part):
    scores = jax.random.randint(key, (EVENTS, SECTORS, 2, HB), 0, 1 << 20) * HB + jnp.arange(HB, dtype=jnp.int32)
    order = jnp.argsort(scores, axis=-1)
    return order[..., :S].astype(jnp.int32)


def set_ends(entries, rng, smallest, top_value):
    dims = entries.shape
    spot = [jax.random.randint(jax.random.fold_in(rng, axis), (), 0, dims[axis]) for axis in range(len(dims))]
    entries = entries.at[tuple(spot)].set(smallest)
    longest = dims.index(max(dims))
    spot[longest] = (spot[longest] + 1) % dims[longest]
    return entries.at[tuple(spot)].set(top_value)


def levels(own_key, dims, split, low, top_value):
    loudness = 1.0
    for position, shards_of in split:
        draws = jax.random.uniform(jax.random.fold_in(jax.random.fold_in(own_key, 6), position), (shards_of,), jnp.float32, low / len(split), top_value / len(split))
        loudness = loudness * jnp.repeat(jnp.exp(draws), dims[position] // shards_of).reshape((-1,) + (1,) * (len(dims) - 1 - position))
    return loudness


def gaussian(rng, extent, spread, most, split=(), kind=jnp.bfloat16):
    entries = spread * jax.random.normal(rng, extent, jnp.float32)
    if split:
        entries = entries * levels(rng, extent, split, -0.22, 0.18)
    return jnp.clip(entries, -most, most).astype(kind)


def setup_inputs(seed: int = 0) -> dict:
    keys = jax.random.split(jax.random.key(seed), 8)
    return {
        "hits": gaussian(keys[0], (EVENTS, ROWS, F), 1.0, 6.0, ((0, 4), (1, 8))),
        "tiles": gaussian(keys[1], (EVENTS, BLOCKS, K, TILE, TILE), (K * TILE) ** -0.5, 0.1875, ((0, 4), (1, 8))),
        "sources": set_ends(jax.random.randint(keys[2], (EVENTS, BLOCKS, K), 0, HB + 2 * S), jax.random.fold_in(keys[2], 1), 0, (HB + 2 * S) - 1).astype(jnp.int32),
        "send_list": draw_send_list(jax.random.fold_in(keys[7], 71), 0),
        "w_message": gaussian(keys[4], (LAYERS, F, F), F ** -0.5, 0.375),
        "w_self": gaussian(keys[5], (LAYERS, F, F), F ** -0.5, 0.375),
        "cotangent": gaussian(keys[6], (EVENTS, ROWS, F), 1.0, 6.0, ((0, 4), (1, 8)), jnp.float32),
    }


def silu_grad(pre):
    sig = jax.nn.sigmoid(pre)
    return sig * (1.0 + pre * (1.0 - sig))

def slot_table(message, send_list):
    blocks = message.reshape(SECTORS, HB, TILE, F)
    from_lower = jnp.take_along_axis(jnp.roll(blocks, 1, 0), jnp.roll(send_list, 1, 0)[:, 0, :, None, None], axis=1)
    from_upper = jnp.take_along_axis(jnp.roll(blocks, -1, 0), jnp.roll(send_list, -1, 0)[:, 1, :, None, None], axis=1)
    return jnp.concatenate([blocks, from_lower, from_upper], axis=1)

def sector_aggregate(args):
    table, sector_sources, sector_tiles = args
    gathered = table[sector_sources].astype(jnp.float32)
    return jnp.einsum('bkij,bkjf->bif', sector_tiles.astype(jnp.float32), gathered)

def sector_slot_grad(args):
    sector_sources, sector_tiles, sector_dpre = args
    contrib = jnp.einsum('bkij,bif->bkjf', sector_tiles.astype(jnp.float32), sector_dpre.astype(jnp.float32))
    empty = jnp.zeros((HB + 2 * S, TILE, F), jnp.float32)
    return empty.at[sector_sources.reshape(-1)].add(contrib.reshape(HB * K, TILE, F))

def add_lent(dblocks, lent_grad, indices):
    return dblocks.at[indices].add(lent_grad)

def one_event(hits, tiles, sources, send_list, w_message, w_self, cotangent):
    tiles_r = tiles.reshape(SECTORS, HB, K, TILE, TILE)
    sources_r = sources.reshape(SECTORS, HB, K)
    current = hits
    saved = []
    for layer_index in range(LAYERS):
        message = jnp.dot(current, w_message[layer_index], preferred_element_type=jnp.float32).astype(jnp.bfloat16)
        table = slot_table(message, send_list)
        aggregate = lax.map(sector_aggregate, (table, sources_r, tiles_r)).reshape(ROWS, F)
        pre = aggregate + jnp.dot(current, w_self[layer_index], preferred_element_type=jnp.float32)
        saved.append((current, pre))
        current = (current.astype(jnp.float32) + jax.nn.silu(pre)).astype(jnp.bfloat16)
    grad = cotangent
    message_steps = [None] * LAYERS
    self_steps = [None] * LAYERS
    for layer_index in reversed(range(LAYERS)):
        layer_in, pre = saved[layer_index]
        dpre = (grad * silu_grad(pre)).astype(jnp.bfloat16)
        slot_grad = lax.map(sector_slot_grad, (sources_r, tiles_r, dpre.reshape(SECTORS, HB, TILE, F)))
        dblocks = slot_grad[:, :HB]
        lower_slots = jnp.roll(slot_grad[:, HB:HB + S], -1, 0)
        upper_slots = jnp.roll(slot_grad[:, HB + S:], 1, 0)
        dblocks = jax.vmap(add_lent)(dblocks, lower_slots, send_list[:, 0])
        dblocks = jax.vmap(add_lent)(dblocks, upper_slots, send_list[:, 1])
        dmessage = dblocks.reshape(ROWS, F).astype(jnp.bfloat16)
        self_steps[layer_index] = jnp.dot(layer_in.T, dpre, preferred_element_type=jnp.float32)
        message_steps[layer_index] = jnp.dot(layer_in.T, dmessage, preferred_element_type=jnp.float32)
        grad = grad + jnp.dot(dpre, w_self[layer_index].T, preferred_element_type=jnp.float32)
        grad = grad + jnp.dot(dmessage, w_message[layer_index].T, preferred_element_type=jnp.float32)
    return (current, grad, jnp.stack(message_steps), jnp.stack(self_steps))

def reference(hits, tiles, sources, send_list, w_message, w_self, cotangent):

    def per_event(args):
        return one_event(args[0], args[1], args[2], args[3], w_message, w_self, args[4])
    outputs, grads, message_steps, self_steps = lax.map(per_event, (hits, tiles, sources, send_list, cotangent))
    scale = 1.0 / jnp.sqrt(jnp.float32(EVENTS * ROWS))
    return (outputs, grads, lax.optimization_barrier(jnp.sum(message_steps, axis=0)) * scale, lax.optimization_barrier(jnp.sum(self_steps, axis=0)) * scale)
```

```python
import functools

import jax
import jax.numpy as jnp
from jax import lax
from jax.experimental import pallas as pl
from jax.experimental.pallas import tpu as pltpu
from jax.sharding import PartitionSpec as P

LAYERS = 2
CHUNK = 256
BF = jnp.bfloat16
F32 = jnp.float32
MESH = pl.DeviceIdType.MESH


def mm(a, b):
    return lax.dot_general(a, b, (((1,), (0,)), ((), ())), preferred_element_type=F32)


def mm_bt(a, b):
    return lax.dot_general(a, b, (((1,), (1,)), ((), ())), preferred_element_type=F32)


def silu_grad(pre):
    sig = jax.nn.sigmoid(pre)
    return sig * (1.0 + pre * (1.0 - sig))


def kernel(
    ndp, nsec, blocks, listed, lent, tile, width, r1, r2,
    pick_ref, lists_ref, back_pos, back_on, hits_hbm, tiles_hbm, cot_hbm, wm_ref, ws_ref,
    hit_out, grad_out, mg_out, sg_out,
    h0, h1, h2, tiles, g, pre0, pre1, msg, a_own, a_halo, halo, lend,
    dpre, dpre_t, dmsg_t, own_t, back_send, back_recv0, back_recv1,
    part, rs1, q1, rs2, r_own, g2, g1,
    load_sem, store_sem, halo_ss, halo_rs, back_ss, back_rs,
    rs1_ss, rs1_rs, rs2_ss, rs2_rs, ag2_ss, ag2_rs, ag1_ss, ag1_rs,
):
    back_recv = (back_recv0, back_recv1)
    rows = blocks * tile
    chunks = rows // CHUNK
    per_chunk = CHUNK // tile
    dp = lax.axis_index("dp")
    sec = lax.axis_index("sector")
    upper = lax.rem(sec + 1, nsec)
    lower = lax.rem(sec + nsec - 1, nsec)
    sec_peers = [lax.rem(sec + o, nsec) for o in range(1, nsec)]
    dp_peers = [lax.rem(dp + o, ndp) for o in range(1, ndp)]
    owners = r1 // r2

    loads = [
        pltpu.make_async_copy(hits_hbm, h0, load_sem.at[0]),
        pltpu.make_async_copy(tiles_hbm, tiles, load_sem.at[1]),
        pltpu.make_async_copy(cot_hbm, g, load_sem.at[2]),
    ]
    for c in loads:
        c.start()

    barrier = pltpu.get_barrier_semaphore()
    for p in sec_peers:
        pl.semaphore_signal(barrier, inc=1, device_id=(dp, p), device_id_type=MESH)
    for p in dp_peers:
        pl.semaphore_signal(barrier, inc=1, device_id=(p, sec), device_id_type=MESH)

    def cond(flag, fn):
        if owners == nsec:
            fn()
        else:
            pl.when(flag)(fn)

    def remote(src, dst, ss, rs, target):
        return pltpu.make_async_remote_copy(
            src_ref=src, dst_ref=dst, send_sem=ss, recv_sem=rs,
            device_id=target, device_id_type=MESH,
        )

    def block_rows(i):
        return pl.ds(pl.multiple_of(i * tile, tile), tile)

    def chunk_rows(i):
        return pl.ds(pl.multiple_of(i * CHUNK, CHUNK), CHUNK)

    def chunk_of(h, i):
        return h[pl.ds(i * per_chunk, per_chunk)].reshape(CHUNK, width)

    def all_of(h):
        return h[...].reshape(rows, width)

    def lent_block(d, i):
        return lists_ref[(sec * 2 + d) * lent + i]

    def send_messages(layer, h):
        copies = []
        for d, target in ((0, upper), (1, lower)):
            for i in range(lent):
                rows_i = h[lent_block(d, i)]
                lend[layer, d, i * tile : (i + 1) * tile, :] = mm(rows_i, wm_ref[layer]).astype(BF)
            c = remote(
                lend.at[layer, d], halo.at[layer, d],
                halo_ss.at[layer, d], halo_rs.at[layer, d], (dp, target),
            )
            c.start()
            copies.append(c)
        return copies

    def own_messages(layer, h):
        @pl.loop(0, chunks)
        def _(i):
            msg[chunk_rows(i), :] = mm(chunk_of(h, i), wm_ref[layer]).astype(BF)

    def own_pre(layer, h, pre):
        @pl.loop(0, chunks)
        def _(i):
            r = chunk_rows(i)
            pre[r, :] = mm(a_own[r, :], msg[...]) + mm(chunk_of(h, i), ws_ref[layer])

    half = lent * tile

    def halo_part(layer, r):
        return mm(a_halo[r, :half], halo[layer, 0]) + mm(a_halo[r, half:], halo[layer, 1])

    def put_dpre(r, i, d):
        dpre[r, :] = d
        for j in range(per_chunk):
            at = pl.ds(pl.multiple_of(i * CHUNK + j * tile, tile), tile)
            dpre_t[:, at] = d[j * tile : (j + 1) * tile, :].T

    loads[0].wait()
    pl.semaphore_wait(barrier, nsec - 1 + ndp - 1)

    sends = send_messages(0, h0)
    own_messages(0, h0)
    loads[1].wait()

    slots = blocks + 2 * lent
    strip = 32

    @pl.loop(0, blocks)
    def _(b):
        for s in range(slots):
            on = [
                jnp.full((16, tile), pick_ref[(b * listed + k) * slots + s], F32).astype(BF)
                for k in range(listed)
            ]
            for j in range(tile // strip):
                cut = slice(j * strip, (j + 1) * strip)
                acc = [
                    tiles[b * listed + k, cut, :] * jnp.concatenate([on[k]] * (strip // 16), axis=0)
                    for k in range(listed)
                ]
                while len(acc) > 1:
                    acc = [x + y for x, y in zip(acc[::2], acc[1::2])]
                at = pl.ds(pl.multiple_of(b * tile + j * strip, strip), strip)
                if s < blocks:
                    a_own[at, s * tile : (s + 1) * tile] = acc[0]
                else:
                    o = s - blocks
                    a_halo[at, o * tile : (o + 1) * tile] = acc[0]

    own_pre(0, h0, pre0)
    for c in sends:
        c.wait()

    @pl.loop(0, chunks)
    def _(i):
        r = chunk_rows(i)
        pre = pre0[r, :] + halo_part(0, r)
        pre0[r, :] = pre
        out = (chunk_of(h0, i).astype(F32) + pre * jax.nn.sigmoid(pre)).astype(BF)
        h1[pl.ds(i * per_chunk, per_chunk)] = out.reshape(per_chunk, tile, width)

    sends = send_messages(1, h1)
    own_messages(1, h1)
    own_pre(1, h1, pre1)

    @pl.loop(0, chunks)
    def _(i):
        r = chunk_rows(i)
        pre0[r, :] = silu_grad(pre0[r, :])

    loads[2].wait()
    for c in sends:
        c.wait()

    @pl.loop(0, chunks)
    def _(i):
        r = chunk_rows(i)
        pre = pre1[r, :] + halo_part(1, r)
        sig = jax.nn.sigmoid(pre)
        h2[r, :] = (chunk_of(h1, i).astype(F32) + pre * sig).astype(BF)
        put_dpre(r, i, (g[r, :] * (sig * (1.0 + pre * (1.0 - sig)))).astype(BF))

    hit_store = pltpu.make_async_copy(h2, hit_out, store_sem.at[0])
    hit_store.start()

    def send_back(layer):
        copies = []
        for d, target in ((0, lower), (1, upper)):
            for i in range(lent // 2):
                lo = (d * lent + 2 * i) * tile
                res = mm(dpre_t[...], a_halo[:, lo : lo + 2 * tile]).astype(BF)
                back_send[layer, d, 2 * i] = res[:, :tile]
                back_send[layer, d, 2 * i + 1] = res[:, tile:]
            c = remote(
                back_send.at[layer, d], back_recv[layer].at[d],
                back_ss.at[layer, d], back_rs.at[layer, d], (dp, target),
            )
            c.start()
            copies.append(c)
        return copies

    def put_part(m, step_t):
        step = step_t.T.astype(BF)
        part[m, :width, :] = step[:, :128]
        part[m, width:, :] = step[:, 128:]

    def own_back(layer, h):
        @pl.loop(0, chunks)
        def _(i):
            own_t[:, chunk_rows(i)] = mm(dpre_t[...], a_own[:, chunk_rows(i)])
            r = chunk_rows(i)
            g[r, :] = g[r, :] + mm_bt(dpre[r, :], ws_ref[layer])

    def finish_back(layer):
        @pl.loop(0, chunks)
        def _(i):
            blocks_t = []
            for j in range(per_chunk):
                b = i * per_chunk + j
                at = block_rows(b)
                total = own_t[:, at]
                for d in range(2):
                    pos = back_pos[d * blocks + b]
                    total = total + back_recv[layer][d, pos].astype(F32) * back_on[d * blocks + b]
                total = total.astype(BF)
                dmsg_t[:, at] = total
                blocks_t.append(total.T)
            r = chunk_rows(i)
            new = g[r, :] + mm_bt(jnp.concatenate(blocks_t, axis=0), wm_ref[layer])
            g[r, :] = new
            if layer == 1:
                put_dpre(r, i, (new * pre0[r, :]).astype(BF))

    bounds = ((0, 3), (3, 1))

    def rs1_start(batch):
        m0, nb = bounds[batch]
        copies = []
        for o, p in enumerate(dp_peers):
            at = pl.ds(pl.multiple_of(p * r1, r1), r1)
            c = remote(
                part.at[pl.ds(m0, nb), at], rs1.at[o, pl.ds(m0, nb)],
                rs1_ss.at[batch, o], rs1_rs.at[batch, o], (p, sec),
            )
            c.start()
            copies.append(c)
        return copies

    def rs2_start(batch, copies):
        m0, nb = bounds[batch]
        for c in copies:
            c.wait()
        own = pl.ds(pl.multiple_of(dp * r1, r1), r1)
        for m in range(m0, m0 + nb):
            total = part[m, own, :].astype(F32)
            for o in range(ndp - 1):
                total = total + rs1[o, m].astype(F32)
            q1[m] = total.astype(BF)
        out = []
        for o, p in enumerate(sec_peers):
            piece = lax.rem(p, owners)
            at = pl.ds(pl.multiple_of(piece * r2, r2), r2)
            c = remote(
                q1.at[pl.ds(m0, nb), at], rs2.at[o, pl.ds(m0, nb)],
                rs2_ss.at[batch, o], rs2_rs.at[batch, o], (dp, p),
            )
            cond(p < owners, c.start)
            out.append((p, c))
        return out

    def ag2_start(batch, copies):
        m0, nb = bounds[batch]
        mine = lax.rem(sec, owners)
        at = pl.ds(pl.multiple_of(mine * r2, r2), r2)
        for p, c in copies:
            cond(p < owners, c.wait_send)
            cond(sec < owners, c.wait_recv)

        def total_up():
            for m in range(m0, m0 + nb):
                total = q1[m, at, :].astype(F32)
                for o in range(nsec - 1):
                    total = total + rs2[o, m].astype(F32)
                r_own[m] = total.astype(BF)
                g2[m, at, :] = r_own[m]

        cond(sec < owners, total_up)
        out = []
        for o, p in enumerate(sec_peers):
            c = remote(
                r_own.at[pl.ds(m0, nb)], g2.at[pl.ds(m0, nb), at],
                ag2_ss.at[batch, o], ag2_rs.at[batch, o], (dp, p),
            )
            cond(sec < owners, c.start)
            source = lax.rem(sec + nsec - 1 - o, nsec)
            out.append((source, c))
        return out

    def ag1_start(batch, copies):
        m0, nb = bounds[batch]
        for source, c in copies:
            cond(sec < owners, c.wait_send)
            cond(source < owners, c.wait_recv)
        at = pl.ds(pl.multiple_of(dp * r1, r1), r1)
        for m in range(m0, m0 + nb):
            g1[m, at, :] = g2[m]
        out = []
        for o, p in enumerate(dp_peers):
            c = remote(
                g2.at[pl.ds(m0, nb)], g1.at[pl.ds(m0, nb), at],
                ag1_ss.at[batch, o], ag1_rs.at[batch, o], (p, sec),
            )
            c.start()
            out.append(c)
        return out

    sends = send_back(1)
    put_part(0, mm(dpre_t[...], all_of(h1)))
    own_back(1, h1)
    for c in sends:
        c.wait()
    finish_back(1)

    sends = send_back(0)
    put_part(1, mm(dmsg_t[...], all_of(h1)))
    put_part(2, mm(dpre_t[...], all_of(h0)))
    first = rs1_start(0)
    own_back(0, h0)
    first = rs2_start(0, first)
    first = ag2_start(0, first)
    for c in sends:
        c.wait()
    finish_back(0)
    put_part(3, mm(dmsg_t[...], all_of(h0)))
    second = rs1_start(1)
    grad_store = pltpu.make_async_copy(g, grad_out, store_sem.at[1])
    grad_store.start()
    first = ag1_start(0, first)
    second = rs2_start(1, second)
    second = ag2_start(1, second)
    second = ag1_start(1, second)
    for c in first + second:
        c.wait()
    for m, out, layer in ((0, sg_out, 1), (1, mg_out, 1), (2, sg_out, 0), (3, mg_out, 0)):
        out[layer, :, :128] = g1[m, :width, :].astype(F32)
        out[layer, :, 128:] = g1[m, width:, :].astype(F32)
    hit_store.wait()
    grad_store.wait()


def per_device(ndp, nsec, hits, tiles, sources, send_list, w_message, w_self, cotangent):
    blocks, listed, tile = tiles.shape[1], tiles.shape[2], tiles.shape[3]
    rows, width = hits.shape[1], hits.shape[2]
    lent = send_list.shape[3]
    folded = 2 * width
    r1 = folded // ndp
    r2 = max(16, r1 // nsec)
    slots = jnp.arange(blocks + 2 * lent, dtype=jnp.int32)
    picks = (sources[0][:, :, None] == slots).astype(F32)
    own_lists = lax.dynamic_index_in_dim(send_list[0], lax.axis_index("sector"), 0, keepdims=False)
    match = own_lists[:, None, :] == slots[:blocks, None]
    back_pos = jnp.sum(match * jnp.arange(lent, dtype=jnp.int32), axis=-1).astype(jnp.int32)
    back_on = jnp.any(match, axis=-1).astype(F32)
    vmem, sem = pltpu.VMEM, pltpu.SemaphoreType.DMA
    scratch = [
        vmem((blocks, tile, width), BF), vmem((blocks, tile, width), BF), vmem((rows, width), BF),
        vmem((blocks * listed, tile, tile), BF),
        vmem((rows, width), F32), vmem((rows, width), F32), vmem((rows, width), F32),
        vmem((rows, width), BF),
        vmem((rows, rows), BF), vmem((rows, 2 * lent * tile), BF),
        vmem((LAYERS, 2, lent * tile, width), BF), vmem((LAYERS, 2, lent * tile, width), BF),
        vmem((rows, width), BF), vmem((width, rows), BF), vmem((width, rows), BF),
        vmem((width, rows), F32),
        vmem((LAYERS, 2, lent, width, tile), BF),
        vmem((2, lent, width, tile), BF), vmem((2, lent, width, tile), BF),
        vmem((4, folded, 128), BF), vmem((ndp - 1, 4, r1, 128), BF), vmem((4, r1, 128), BF),
        vmem((nsec - 1, 4, r2, 128), BF), vmem((4, r2, 128), BF), vmem((4, r1, 128), BF),
        vmem((4, folded, 128), BF),
        sem((3,)), sem((2,)), sem((LAYERS, 2)), sem((LAYERS, 2)), sem((LAYERS, 2)), sem((LAYERS, 2)),
        sem((2, ndp - 1)), sem((2, ndp - 1)), sem((2, nsec - 1)), sem((2, nsec - 1)),
        sem((2, nsec - 1)), sem((2, nsec - 1)), sem((2, ndp - 1)), sem((2, ndp - 1)),
    ]
    flat = pl.BlockSpec(memory_space=pltpu.SMEM)
    far = pl.BlockSpec(memory_space=pl.ANY)
    near = pl.BlockSpec(memory_space=pltpu.VMEM)
    hit_output, grad, message_total, self_total = pl.pallas_call(
        functools.partial(kernel, ndp, nsec, blocks, listed, lent, tile, width, r1, r2),
        out_shape=(
            jax.ShapeDtypeStruct((rows, width), BF),
            jax.ShapeDtypeStruct((rows, width), F32),
            jax.ShapeDtypeStruct(w_message.shape, F32),
            jax.ShapeDtypeStruct(w_self.shape, F32),
        ),
        in_specs=[flat, flat, flat, flat, far, far, far, near, near],
        out_specs=(far, far, near, near),
        scratch_shapes=scratch,
        compiler_params=pltpu.CompilerParams(
            collective_id=0, has_side_effects=True, vmem_limit_bytes=56 * 1024 * 1024
        ),
    )(
        picks.reshape(-1), send_list.reshape(-1), back_pos.reshape(-1), back_on.reshape(-1),
        hits[0].reshape(blocks, tile, width),
        tiles.reshape(blocks * listed, tile, tile), cotangent[0], w_message, w_self,
    )
    total_rows = rows * ndp * nsec
    scale = 1.0 / jnp.sqrt(jnp.float32(total_rows))
    return (hit_output[None], grad[None], message_total * scale, self_total * scale)


def solution(mesh):
    in_specs = (
        P("dp", "sector", None),
        P("dp", "sector", None, None, None),
        P("dp", "sector", None),
        P("dp", None, None, None),
        P(),
        P(),
        P("dp", "sector", None),
    )
    out_specs = (P("dp", "sector", None), P("dp", "sector", None), P(), P())
    return jax.shard_map(
        functools.partial(per_device, mesh.shape["dp"], mesh.shape["sector"]),
        mesh=mesh, in_specs=in_specs, out_specs=out_specs, check_vma=False,
    )
```

```python
import functools

import jax
import jax.numpy as jnp
from jax import lax
from jax.experimental import pallas as pl
from jax.experimental.pallas import tpu as pltpu
from jax.sharding import PartitionSpec as P

LAYERS = 2
CHUNK = 256
BF = jnp.bfloat16
F32 = jnp.float32
MESH = pl.DeviceIdType.MESH


def mm(a, b):
    return lax.dot_general(a, b, (((1,), (0,)), ((), ())), preferred_element_type=F32)


def mm_bt(a, b):
    return lax.dot_general(a, b, (((1,), (1,)), ((), ())), preferred_element_type=F32)


def silu_grad(pre):
    sig = jax.nn.sigmoid(pre)
    return sig * (1.0 + pre * (1.0 - sig))


def kernel(
    ndp, nsec, blocks, listed, lent, tile, width, r1, r2,
    table, hits_hbm, tiles_hbm, cot_hbm, wm_hbm, ws_hbm,
    hit_out, grad_out, mg_out, sg_out,
    h0, h1, h2, tiles, g, wm_ref, ws_ref, pre0, pre1, msg, hmsg, a_own, a_halo, halo, lend,
    dpre, dpre_t, dmsg_t, own_t, back_send, back_recv0, back_recv1,
    part, rs1, q1, rs2, r_own, g2, g1,
    load_sem, store_sem, halo_ss, halo_rs, back_ss, back_rs,
    rs1_ss, rs1_rs, rs2_ss, rs2_rs, ag2_ss, ag2_rs, ag1_ss, ag1_rs,
):
    back_recv = (back_recv0, back_recv1)
    rows = blocks * tile
    chunks = rows // CHUNK
    per_chunk = CHUNK // tile
    dp = lax.axis_index("dp")
    sec = lax.axis_index("sector")
    upper = lax.rem(sec + 1, nsec)
    lower = lax.rem(sec + nsec - 1, nsec)
    sec_peers = [lax.rem(sec + o, nsec) for o in range(1, nsec)]
    dp_peers = [lax.rem(dp + o, ndp) for o in range(1, ndp)]
    owners = r1 // r2

    loads = [
        pltpu.make_async_copy(hits_hbm, h0, load_sem.at[0]),
        pltpu.make_async_copy(wm_hbm, wm_ref, load_sem.at[1]),
        pltpu.make_async_copy(tiles_hbm, tiles.at[pl.ds(0, blocks * listed)], load_sem.at[2]),
        pltpu.make_async_copy(ws_hbm, ws_ref, load_sem.at[3]),
        pltpu.make_async_copy(cot_hbm, g, load_sem.at[4]),
    ]
    for c in loads:
        c.start()

    barrier = pltpu.get_barrier_semaphore()
    for p in sec_peers:
        pl.semaphore_signal(barrier, inc=1, device_id=(dp, p), device_id_type=MESH)
    for p in dp_peers:
        pl.semaphore_signal(barrier, inc=1, device_id=(p, sec), device_id_type=MESH)

    def cond(flag, fn):
        if owners == nsec:
            fn()
        else:
            pl.when(flag)(fn)

    def remote(src, dst, ss, rs, target):
        return pltpu.make_async_remote_copy(
            src_ref=src, dst_ref=dst, send_sem=ss, recv_sem=rs,
            device_id=target, device_id_type=MESH,
        )

    def block_rows(i):
        return pl.ds(pl.multiple_of(i * tile, tile), tile)

    def chunk_rows(i):
        return pl.ds(pl.multiple_of(i * CHUNK, CHUNK), CHUNK)

    def chunk_of(h, i):
        return h[pl.ds(i * per_chunk, per_chunk)].reshape(CHUNK, width)

    def all_of(h):
        return h[...].reshape(rows, width)

    def lent_block(d, i):
        return table[d * lent + i]

    def send_lent(layer, make):
        copies = []
        for d, target in ((0, upper), (1, lower)):
            lend[layer, d] = make([lent_block(d, i) for i in range(lent)])
            c = remote(
                lend.at[layer, d], halo.at[layer, d],
                halo_ss.at[layer, d], halo_rs.at[layer, d], (dp, target),
            )
            c.start()
            copies.append(c)
        return copies

    def own_messages(layer, h):
        @pl.loop(0, chunks)
        def _(i):
            msg[chunk_rows(i), :] = mm(chunk_of(h, i), wm_ref[layer]).astype(BF)

    def own_pre(layer, h, pre):
        @pl.loop(0, chunks)
        def _(i):
            r = chunk_rows(i)
            out = mm(a_own[r, :], msg[...]) + mm(chunk_of(h, i), ws_ref[layer])
            pre[pl.ds(i * per_chunk, per_chunk)] = out.reshape(per_chunk, tile, width)

    half = lent * tile

    def halo_messages(layer):
        for d in range(2):
            hmsg[d * half : (d + 1) * half, :] = mm(halo[layer, d], wm_ref[layer]).astype(BF)

    def halo_part(i):
        rows_a = a_halo[pl.ds(i * per_chunk, per_chunk)].reshape(CHUNK, 2 * half)
        return mm(rows_a, hmsg[...])

    def put_dpre(r, i, d):
        dpre[r, :] = d
        for j in range(per_chunk):
            at = pl.ds(pl.multiple_of(i * CHUNK + j * tile, tile), tile)
            dpre_t[:, at] = d[j * tile : (j + 1) * tile, :].T

    loads[0].wait()
    pl.semaphore_wait(barrier, nsec - 1 + ndp - 1)

    sends = send_lent(0, lambda ids: jnp.concatenate([h0[b] for b in ids], axis=0))
    loads[1].wait()
    own_messages(0, h0)
    tiles[blocks * listed] = jnp.zeros((tile, tile), BF)
    back_recv0[:, lent] = jnp.zeros((2, width, tile), BF)
    back_recv1[:, lent] = jnp.zeros((2, width, tile), BF)
    loads[2].wait()

    slots = blocks + 2 * lent
    at_first = 2 * lent + 2 * blocks
    at_next = at_first + blocks * slots

    @pl.loop(0, blocks)
    def _(b):
        for k in reversed(range(listed - 1)):
            e = b * listed + k
            tiles[e] = tiles[e] + tiles[table[at_next + e]]
        for s in range(slots):
            val = tiles[table[at_first + b * slots + s]]
            if s < blocks:
                a_own[block_rows(b), s * tile : (s + 1) * tile] = val
            else:
                o = s - blocks
                a_halo[b, :, o * tile : (o + 1) * tile] = val

    loads[3].wait()
    own_pre(0, h0, pre0)
    for c in sends:
        c.wait()
    halo_messages(0)

    def layer_out(h, pre):
        return (h.astype(F32) + pre * jax.nn.sigmoid(pre)).astype(BF)

    def lent_out(ids):
        pre = jnp.concatenate([pre0[b] for b in ids], axis=0)
        pre = pre + mm(jnp.concatenate([a_halo[b] for b in ids], axis=0), hmsg[...])
        return layer_out(jnp.concatenate([h0[b] for b in ids], axis=0), pre)

    sends = send_lent(1, lent_out)

    @pl.loop(0, chunks)
    def _(i):
        at = pl.ds(i * per_chunk, per_chunk)
        pre = chunk_of(pre0, i) + halo_part(i)
        h1[at] = layer_out(chunk_of(h0, i), pre).reshape(per_chunk, tile, width)
        pre0[at] = silu_grad(pre).reshape(per_chunk, tile, width)

    own_messages(1, h1)
    own_pre(1, h1, pre1)
    loads[4].wait()
    for c in sends:
        c.wait()
    halo_messages(1)

    @pl.loop(0, chunks)
    def _(i):
        r = chunk_rows(i)
        pre = chunk_of(pre1, i) + halo_part(i)
        sig = jax.nn.sigmoid(pre)
        h2[r, :] = (chunk_of(h1, i).astype(F32) + pre * sig).astype(BF)
        put_dpre(r, i, (g[r, :] * (sig * (1.0 + pre * (1.0 - sig)))).astype(BF))

    hit_store = pltpu.make_async_copy(h2, hit_out, store_sem.at[0])
    hit_store.start()

    def send_back(layer):
        copies = []
        for d, target in ((0, lower), (1, upper)):
            for i in range(lent // 2):
                lo = (d * lent + 2 * i) * tile
                a_cols = a_halo[:, :, lo : lo + 2 * tile].reshape(rows, 2 * tile)
                res = mm(dpre_t[...], a_cols).astype(BF)
                back_send[layer, d, 2 * i] = res[:, :tile]
                back_send[layer, d, 2 * i + 1] = res[:, tile:]
                c = remote(
                    back_send.at[layer, d, pl.ds(2 * i, 2)], back_recv[layer].at[d, pl.ds(2 * i, 2)],
                    back_ss.at[layer, d, i], back_rs.at[layer, d, i], (dp, target),
                )
                c.start()
                copies.append(c)
        return copies

    def put_part(m, step_t):
        step = step_t.T.astype(BF)
        part[m, :width, :] = step[:, :128]
        part[m, width:, :] = step[:, 128:]

    def own_back(layer, h):
        @pl.loop(0, chunks)
        def _(i):
            out = mm(dpre_t[...], a_own[:, chunk_rows(i)])
            own_t[:, chunk_rows(i)] = out
            dmsg_t[:, chunk_rows(i)] = out.astype(BF)
            r = chunk_rows(i)
            g[r, :] = g[r, :] + mm_bt(dpre[r, :], ws_ref[layer])

    def message_part(layer, h):
        total = mm(dmsg_t[...], all_of(h))
        for d in range(2):
            for i in range(lent):
                total = total + mm(back_send[layer, d, i], halo[layer, d, i * tile : (i + 1) * tile, :])
        return total

    def finish_back(layer):
        @pl.loop(0, chunks)
        def _(i):
            blocks_t = []
            for j in range(per_chunk):
                b = i * per_chunk + j
                at = block_rows(b)
                total = own_t[:, at]
                for d in range(2):
                    pos = table[2 * lent + d * blocks + b]
                    total = total + back_recv[layer][d, pos].astype(F32)
                total = total.astype(BF)
                blocks_t.append(total.T)
            r = chunk_rows(i)
            new = g[r, :] + mm_bt(jnp.concatenate(blocks_t, axis=0), wm_ref[layer])
            g[r, :] = new
            if layer == 1:
                put_dpre(r, i, (new * chunk_of(pre0, i)).astype(BF))

    bounds = ((0, 2), (2, 2))

    def rs1_start(batch):
        m0, nb = bounds[batch]
        copies = []
        for o, p in enumerate(dp_peers):
            at = pl.ds(pl.multiple_of(p * r1, r1), r1)
            c = remote(
                part.at[pl.ds(m0, nb), at], rs1.at[o, pl.ds(m0, nb)],
                rs1_ss.at[batch, o], rs1_rs.at[batch, o], (p, sec),
            )
            c.start()
            copies.append(c)
        return copies

    def rs2_start(batch, copies):
        m0, nb = bounds[batch]
        for c in copies:
            c.wait()
        own = pl.ds(pl.multiple_of(dp * r1, r1), r1)
        for m in range(m0, m0 + nb):
            total = part[m, own, :].astype(F32)
            for o in range(ndp - 1):
                total = total + rs1[o, m].astype(F32)
            q1[m] = total.astype(BF)
        out = []
        for o, p in enumerate(sec_peers):
            piece = lax.rem(p, owners)
            at = pl.ds(pl.multiple_of(piece * r2, r2), r2)
            c = remote(
                q1.at[pl.ds(m0, nb), at], rs2.at[o, pl.ds(m0, nb)],
                rs2_ss.at[batch, o], rs2_rs.at[batch, o], (dp, p),
            )
            cond(p < owners, c.start)
            out.append((p, c))
        return out

    def ag2_start(batch, copies):
        m0, nb = bounds[batch]
        mine = lax.rem(sec, owners)
        at = pl.ds(pl.multiple_of(mine * r2, r2), r2)
        for p, c in copies:
            cond(p < owners, c.wait_send)
            cond(sec < owners, c.wait_recv)

        def total_up():
            for m in range(m0, m0 + nb):
                total = q1[m, at, :].astype(F32)
                for o in range(nsec - 1):
                    total = total + rs2[o, m].astype(F32)
                r_own[m] = total.astype(BF)
                g2[m, at, :] = r_own[m]

        cond(sec < owners, total_up)
        out = []
        for o, p in enumerate(sec_peers):
            c = remote(
                r_own.at[pl.ds(m0, nb)], g2.at[pl.ds(m0, nb), at],
                ag2_ss.at[batch, o], ag2_rs.at[batch, o], (dp, p),
            )
            cond(sec < owners, c.start)
            source = lax.rem(sec + nsec - 1 - o, nsec)
            out.append((source, c))
        return out

    def ag1_start(batch, copies):
        m0, nb = bounds[batch]
        for source, c in copies:
            cond(sec < owners, c.wait_send)
            cond(source < owners, c.wait_recv)
        at = pl.ds(pl.multiple_of(dp * r1, r1), r1)
        for m in range(m0, m0 + nb):
            g1[m, at, :] = g2[m]
        out = []
        for o, p in enumerate(dp_peers):
            c = remote(
                g2.at[pl.ds(m0, nb)], g1.at[pl.ds(m0, nb), at],
                ag1_ss.at[batch, o], ag1_rs.at[batch, o], (p, sec),
            )
            c.start()
            out.append(c)
        return out

    sends = send_back(1)
    put_part(0, mm(dpre_t[...], all_of(h1)))
    own_back(1, h1)
    put_part(1, message_part(1, h1))
    first = rs1_start(0)
    first = rs2_start(0, first)
    first = ag2_start(0, first)
    for c in sends:
        c.wait()
    finish_back(1)

    sends = send_back(0)
    put_part(2, mm(dpre_t[...], all_of(h0)))
    own_back(0, h0)
    put_part(3, message_part(0, h0))
    second = rs1_start(1)
    first = ag1_start(0, first)
    second = rs2_start(1, second)
    second = ag2_start(1, second)
    for c in sends:
        c.wait()
    finish_back(0)
    grad_store = pltpu.make_async_copy(g, grad_out, store_sem.at[1])
    grad_store.start()
    second = ag1_start(1, second)
    for c in first + second:
        c.wait()
    scale = 1.0 / (float(rows * ndp * nsec) ** 0.5)
    for m, out, layer in ((0, sg_out, 1), (1, mg_out, 1), (2, sg_out, 0), (3, mg_out, 0)):
        out[layer, :, :128] = g1[m, :width, :].astype(F32) * scale
        out[layer, :, 128:] = g1[m, width:, :].astype(F32) * scale
    hit_store.wait()
    grad_store.wait()


def per_device(ndp, nsec, hits, tiles, sources, send_list, w_message, w_self, cotangent):
    blocks, listed, tile = tiles.shape[1], tiles.shape[2], tiles.shape[3]
    rows, width = hits.shape[1], hits.shape[2]
    lent = send_list.shape[3]
    folded = 2 * width
    r1 = folded // ndp
    r2 = max(16, r1 // nsec)
    own_lists = lax.dynamic_index_in_dim(send_list[0], lax.axis_index("sector"), 0, keepdims=False)
    places = jnp.arange(blocks + 2 * lent, dtype=jnp.int32)
    turn = jnp.arange(lent, dtype=jnp.int32)
    match = own_lists[:, None, :] == places[:blocks, None]
    back_pos = jnp.min(jnp.where(match, turn, lent), axis=-1)
    ids = sources[0]
    order = jnp.arange(listed, dtype=jnp.int32)
    entry = jnp.arange(blocks, dtype=jnp.int32)[:, None] * listed
    none = blocks * listed
    first = jnp.min(
        jnp.where(ids[:, None, :] == places[:, None], entry[:, :, None] + order, none), axis=-1
    )
    later = (ids[:, None, :] == ids[:, :, None]) & (order > order[:, None])
    following = jnp.min(jnp.where(later, entry[:, :, None] + order, none), axis=-1)
    table = jnp.concatenate(
        [own_lists.reshape(-1), back_pos.reshape(-1), first.reshape(-1), following.reshape(-1)]
    ).astype(jnp.int32)
    vmem, sem = pltpu.VMEM, pltpu.SemaphoreType.DMA
    scratch = [
        vmem((blocks, tile, width), BF), vmem((blocks, tile, width), BF), vmem((rows, width), BF),
        vmem((blocks * listed + 1, tile, tile), BF), vmem((rows, width), F32),
        vmem(w_message.shape, BF), vmem(w_self.shape, BF),
        vmem((blocks, tile, width), F32), vmem((blocks, tile, width), F32),
        vmem((rows, width), BF), vmem((2 * lent * tile, width), BF),
        vmem((rows, rows), BF), vmem((blocks, tile, 2 * lent * tile), BF),
        vmem((LAYERS, 2, lent * tile, width), BF), vmem((LAYERS, 2, lent * tile, width), BF),
        vmem((rows, width), BF), vmem((width, rows), BF), vmem((width, rows), BF),
        vmem((width, rows), F32),
        vmem((LAYERS, 2, lent, width, tile), BF),
        vmem((2, lent + 1, width, tile), BF), vmem((2, lent + 1, width, tile), BF),
        vmem((4, folded, 128), BF), vmem((ndp - 1, 4, r1, 128), BF), vmem((4, r1, 128), BF),
        vmem((nsec - 1, 4, r2, 128), BF), vmem((4, r2, 128), BF), vmem((4, r1, 128), BF),
        vmem((4, folded, 128), BF),
        sem((5,)), sem((2,)), sem((LAYERS, 2)), sem((LAYERS, 2)),
        sem((LAYERS, 2, lent // 2)), sem((LAYERS, 2, lent // 2)),
        sem((2, ndp - 1)), sem((2, ndp - 1)), sem((2, nsec - 1)), sem((2, nsec - 1)),
        sem((2, nsec - 1)), sem((2, nsec - 1)), sem((2, ndp - 1)), sem((2, ndp - 1)),
    ]
    flat = pl.BlockSpec(memory_space=pltpu.SMEM)
    far = pl.BlockSpec(memory_space=pl.ANY)
    near = pl.BlockSpec(memory_space=pltpu.VMEM)
    hit_output, grad, message_total, self_total = pl.pallas_call(
        functools.partial(kernel, ndp, nsec, blocks, listed, lent, tile, width, r1, r2),
        out_shape=(
            jax.ShapeDtypeStruct((rows, width), BF),
            jax.ShapeDtypeStruct((rows, width), F32),
            jax.ShapeDtypeStruct(w_message.shape, F32),
            jax.ShapeDtypeStruct(w_self.shape, F32),
        ),
        in_specs=[flat, far, far, far, far, far],
        out_specs=(far, far, near, near),
        scratch_shapes=scratch,
        compiler_params=pltpu.CompilerParams(
            collective_id=0, has_side_effects=True, vmem_limit_bytes=56 * 1024 * 1024
        ),
    )(
        table, hits[0].reshape(blocks, tile, width),
        tiles.reshape(blocks * listed, tile, tile), cotangent[0], w_message, w_self,
    )
    return (hit_output[None], grad[None], message_total, self_total)


def solution(mesh):
    in_specs = (
        P("dp", "sector", None),
        P("dp", "sector", None, None, None),
        P("dp", "sector", None),
        P("dp", None, None, None),
        P(),
        P(),
        P("dp", "sector", None),
    )
    out_specs = (P("dp", "sector", None), P("dp", "sector", None), P(), P())
    return jax.shard_map(
        functools.partial(per_device, mesh.shape["dp"], mesh.shape["sector"]),
        mesh=mesh, in_specs=in_specs, out_specs=out_specs, check_vma=False,
    )
```

```python
import functools

import jax
import jax.numpy as jnp
from jax import lax
from jax.experimental import pallas as pl
from jax.experimental.pallas import tpu as pltpu
from jax.sharding import PartitionSpec as P

LAYERS = 2
CHUNK = 256
BF = jnp.bfloat16
F32 = jnp.float32
MESH = pl.DeviceIdType.MESH


def mm(a, b):
    return lax.dot_general(a, b, (((1,), (0,)), ((), ())), preferred_element_type=F32)


def silu_grad(pre):
    sig = jax.nn.sigmoid(pre)
    return sig * (1.0 + pre * (1.0 - sig))


def kernel(
    ndp, nsec, blocks, listed, lent, tile, width, r1, r2,
    src_ref, lists_ref, hits_hbm, tiles_hbm, cot_hbm, wm_hbm, ws_hbm,
    hit_out, grad_out, mg_out, sg_out,
    h0, h1, h2, tiles, g, wm_ref, ws_ref, pre0, pre1, msg, hmsg, a_own, a_halo, halo, lend,
    g_t, sg_t, dpre_t, dmsg_t, own_t, back_send, back_recv0, back_recv1,
    part, rs1, q1, rs2, r_own, g2, g1,
    load_sem, store_sem, halo_ss, halo_rs, back_ss, back_rs,
    rs1_ss, rs1_rs, rs2_ss, rs2_rs, ag2_ss, ag2_rs, ag1_ss, ag1_rs,
):
    back_recv = (back_recv0, back_recv1)
    rows = blocks * tile
    chunks = rows // CHUNK
    per_chunk = CHUNK // tile
    dp = lax.axis_index("dp")
    sec = lax.axis_index("sector")
    upper = lax.rem(sec + 1, nsec)
    lower = lax.rem(sec + nsec - 1, nsec)
    sec_peers = [lax.rem(sec + o, nsec) for o in range(1, nsec)]
    dp_peers = [lax.rem(dp + o, ndp) for o in range(1, ndp)]
    owners = r1 // r2

    loads = [
        pltpu.make_async_copy(hits_hbm, h0, load_sem.at[0]),
        pltpu.make_async_copy(wm_hbm, wm_ref, load_sem.at[1]),
        pltpu.make_async_copy(tiles_hbm, tiles.at[pl.ds(0, blocks * listed)], load_sem.at[2]),
        pltpu.make_async_copy(ws_hbm, ws_ref, load_sem.at[3]),
        pltpu.make_async_copy(cot_hbm, g, load_sem.at[4]),
    ]
    for c in loads:
        c.start()

    barrier = pltpu.get_barrier_semaphore()
    for p in sec_peers:
        pl.semaphore_signal(barrier, inc=1, device_id=(dp, p), device_id_type=MESH)
    for p in dp_peers:
        pl.semaphore_signal(barrier, inc=1, device_id=(p, sec), device_id_type=MESH)

    def cond(flag, fn):
        if owners == nsec:
            fn()
        else:
            pl.when(flag)(fn)

    def remote(src, dst, ss, rs, target):
        return pltpu.make_async_remote_copy(
            src_ref=src, dst_ref=dst, send_sem=ss, recv_sem=rs,
            device_id=target, device_id_type=MESH,
        )

    def block_rows(i):
        return pl.ds(pl.multiple_of(i * tile, tile), tile)

    def chunk_rows(i):
        return pl.ds(pl.multiple_of(i * CHUNK, CHUNK), CHUNK)

    def chunk_of(h, i):
        return h[pl.ds(i * per_chunk, per_chunk)].reshape(CHUNK, width)

    def all_of(h):
        return h[...].reshape(rows, width)

    def lent_block(d, i):
        return lists_ref[sec, d, i]

    def send_lent(layer, make):
        copies = []
        for d, target in ((0, upper), (1, lower)):
            if make is not None:
                lend[layer, d] = make([lent_block(d, i) for i in range(lent)])
            c = remote(
                lend.at[layer, d], halo.at[layer, d],
                halo_ss.at[layer, d], halo_rs.at[layer, d], (dp, target),
            )
            c.start()
            copies.append(c)
        return copies

    def own_messages(layer, h):
        @pl.loop(0, chunks)
        def _(i):
            msg[chunk_rows(i), :] = mm(chunk_of(h, i), wm_ref[layer]).astype(BF)

    def own_pre(layer, h, pre):
        @pl.loop(0, chunks)
        def _(i):
            r = chunk_rows(i)
            out = mm(a_own[r, :], msg[...]) + mm(chunk_of(h, i), ws_ref[layer])
            pre[pl.ds(i * per_chunk, per_chunk)] = out.reshape(per_chunk, tile, width)

    half = lent * tile

    def halo_messages(layer):
        for d in range(2):
            hmsg[d * half : (d + 1) * half, :] = mm(halo[layer, d], wm_ref[layer]).astype(BF)

    def halo_part(i):
        rows_a = a_halo[pl.ds(i * per_chunk, per_chunk)].reshape(CHUNK, 2 * half)
        return mm(rows_a, hmsg[...])

    def put_turned(dst, i, d):
        for j in range(per_chunk):
            at = pl.ds(pl.multiple_of(i * CHUNK + j * tile, tile), tile)
            dst[:, at] = d[j * tile : (j + 1) * tile, :].T

    loads[0].wait()
    for d in range(2):
        lend[0, d] = jnp.concatenate([h0[lent_block(d, i)] for i in range(lent)], axis=0)
    pl.semaphore_wait(barrier, nsec - 1 + ndp - 1)

    sends = send_lent(0, None)
    loads[1].wait()
    own_messages(0, h0)
    tiles[blocks * listed] = jnp.zeros((tile, tile), BF)
    back_recv0[:, lent] = jnp.zeros((2, width, tile), BF)
    back_recv1[:, lent] = jnp.zeros((2, width, tile), BF)
    loads[2].wait()

    slots = blocks + 2 * lent
    none = blocks * listed

    def least(pairs):
        best = jnp.int32(none)
        for index, away in pairs:
            best = jnp.minimum(best, index + none * (away * away))
        return best

    @pl.loop(0, blocks)
    def _(b):
        base = b * listed
        ids = [src_ref[b, k] for k in range(listed)]
        for k in reversed(range(listed - 1)):
            later = least([(base + m, ids[m] - ids[k]) for m in range(k + 1, listed)])
            tiles[base + k] = tiles[base + k] + tiles[later]
        for s in range(slots):
            val = tiles[least([(base + k, ids[k] - s) for k in range(listed)])]
            if s < blocks:
                a_own[block_rows(b), s * tile : (s + 1) * tile] = val
            else:
                o = s - blocks
                a_halo[b, :, o * tile : (o + 1) * tile] = val

    loads[3].wait()
    own_pre(0, h0, pre0)
    for c in sends:
        c.wait()
    halo_messages(0)

    def layer_out(h, pre):
        return (h.astype(F32) + pre * jax.nn.sigmoid(pre)).astype(BF)

    def lent_out(ids):
        pre = jnp.concatenate([pre0[b] for b in ids], axis=0)
        pre = pre + mm(jnp.concatenate([a_halo[b] for b in ids], axis=0), hmsg[...])
        return layer_out(jnp.concatenate([h0[b] for b in ids], axis=0), pre)

    sends = send_lent(1, lent_out)

    @pl.loop(0, chunks)
    def _(i):
        at = pl.ds(i * per_chunk, per_chunk)
        pre = chunk_of(pre0, i) + halo_part(i)
        h1[at] = layer_out(chunk_of(h0, i), pre).reshape(per_chunk, tile, width)
        put_turned(sg_t, i, silu_grad(pre))

    own_messages(1, h1)
    own_pre(1, h1, pre1)
    loads[4].wait()

    @pl.loop(0, chunks)
    def _(i):
        put_turned(g_t, i, g[chunk_rows(i), :])

    for c in sends:
        c.wait()
    halo_messages(1)

    @pl.loop(0, chunks, unroll=2)
    def _(i):
        r = chunk_rows(i)
        pre = chunk_of(pre1, i) + halo_part(i)
        sig = jax.nn.sigmoid(pre)
        h2[r, :] = (chunk_of(h1, i).astype(F32) + pre * sig).astype(BF)
        put_turned(dpre_t, i, (g[r, :] * (sig * (1.0 + pre * (1.0 - sig)))).astype(BF))

    hit_store = pltpu.make_async_copy(h2, hit_out, store_sem.at[0])
    hit_store.start()

    def send_back(layer):
        copies = []
        for d, target in ((0, lower), (1, upper)):
            for i in range(lent // 2):
                lo = (d * lent + 2 * i) * tile
                a_cols = a_halo[:, :, lo : lo + 2 * tile].reshape(rows, 2 * tile)
                res = mm(dpre_t[...], a_cols).astype(BF)
                back_send[layer, d, 2 * i] = res[:, :tile]
                back_send[layer, d, 2 * i + 1] = res[:, tile:]
                c = remote(
                    back_send.at[layer, d, pl.ds(2 * i, 2)], back_recv[layer].at[d, pl.ds(2 * i, 2)],
                    back_ss.at[layer, d, i], back_rs.at[layer, d, i], (dp, target),
                )
                c.start()
                copies.append(c)
        return copies

    def put_part(m, step_t):
        step = step_t.T.astype(BF)
        part[m, :width, :] = step[:, :128]
        part[m, width:, :] = step[:, 128:]

    def own_back(layer, h):
        @pl.loop(0, chunks)
        def _(i):
            out = mm(dpre_t[...], a_own[:, chunk_rows(i)])
            own_t[:, chunk_rows(i)] = out
            dmsg_t[:, chunk_rows(i)] = out.astype(BF)
            c = chunk_rows(i)
            g_t[:, c] = g_t[:, c] + mm(ws_ref[layer], dpre_t[:, c])

    def message_part(layer, h):
        total = mm(dmsg_t[...], all_of(h))
        for d in range(2):
            for i in range(lent):
                total = total + mm(back_send[layer, d, i], halo[layer, d, i * tile : (i + 1) * tile, :])
        return total

    def finish_back(layer, lo, hi):
        @pl.loop(lo, hi, unroll=2)
        def _(i):
            c = chunk_rows(i)
            lent_sum = []
            for j in range(per_chunk):
                b = i * per_chunk + j
                total = jnp.zeros((width, tile), F32)
                for d in range(2):
                    pos = jnp.int32(lent)
                    for k in range(lent):
                        away = lent_block(d, k) - b
                        pos = jnp.minimum(pos, k + lent * (away * away))
                    total = total + back_recv[layer][d, pos].astype(F32)
                lent_sum.append(total)
            total = (own_t[:, c] + jnp.concatenate(lent_sum, axis=1)).astype(BF)
            new = g_t[:, c] + mm(wm_ref[layer], total)
            if layer > 0:
                g_t[:, c] = new
                dpre_t[:, c] = (new * sg_t[:, c]).astype(BF)
            else:
                g[c, :] = new.T

    bounds = ((0, 2), (2, 2))

    def rs1_start(batch):
        m0, nb = bounds[batch]
        copies = []
        for o, p in enumerate(dp_peers):
            at = pl.ds(pl.multiple_of(p * r1, r1), r1)
            c = remote(
                part.at[pl.ds(m0, nb), at], rs1.at[o, pl.ds(m0, nb)],
                rs1_ss.at[batch, o], rs1_rs.at[batch, o], (p, sec),
            )
            c.start()
            copies.append(c)
        return copies

    def rs2_start(batch, copies):
        m0, nb = bounds[batch]
        for c in copies:
            c.wait()
        own = pl.ds(pl.multiple_of(dp * r1, r1), r1)
        for m in range(m0, m0 + nb):
            total = part[m, own, :].astype(F32)
            for o in range(ndp - 1):
                total = total + rs1[o, m].astype(F32)
            q1[m] = total.astype(BF)
        out = []
        for o, p in enumerate(sec_peers):
            piece = lax.rem(p, owners)
            at = pl.ds(pl.multiple_of(piece * r2, r2), r2)
            c = remote(
                q1.at[pl.ds(m0, nb), at], rs2.at[o, pl.ds(m0, nb)],
                rs2_ss.at[batch, o], rs2_rs.at[batch, o], (dp, p),
            )
            cond(p < owners, c.start)
            out.append((p, c))
        return out

    def ag2_start(batch, copies):
        m0, nb = bounds[batch]
        mine = lax.rem(sec, owners)
        at = pl.ds(pl.multiple_of(mine * r2, r2), r2)
        for p, c in copies:
            cond(p < owners, c.wait_send)
            cond(sec < owners, c.wait_recv)

        def total_up():
            for m in range(m0, m0 + nb):
                total = q1[m, at, :].astype(F32)
                for o in range(nsec - 1):
                    total = total + rs2[o, m].astype(F32)
                r_own[m] = total.astype(BF)
                g2[m, at, :] = r_own[m]

        cond(sec < owners, total_up)
        out = []
        for o, p in enumerate(sec_peers):
            c = remote(
                r_own.at[pl.ds(m0, nb)], g2.at[pl.ds(m0, nb), at],
                ag2_ss.at[batch, o], ag2_rs.at[batch, o], (dp, p),
            )
            cond(sec < owners, c.start)
            source = lax.rem(sec + nsec - 1 - o, nsec)
            out.append((source, c))
        return out

    def ag1_start(batch, copies):
        m0, nb = bounds[batch]
        for source, c in copies:
            cond(sec < owners, c.wait_send)
            cond(source < owners, c.wait_recv)
        at = pl.ds(pl.multiple_of(dp * r1, r1), r1)
        for m in range(m0, m0 + nb):
            g1[m, at, :] = g2[m]
        out = []
        for o, p in enumerate(dp_peers):
            c = remote(
                g2.at[pl.ds(m0, nb)], g1.at[pl.ds(m0, nb), at],
                ag1_ss.at[batch, o], ag1_rs.at[batch, o], (p, sec),
            )
            c.start()
            out.append(c)
        return out

    sends = send_back(1)
    put_part(0, mm(dpre_t[...], all_of(h1)))
    own_back(1, h1)
    put_part(1, message_part(1, h1))
    first = rs1_start(0)
    first = rs2_start(0, first)
    first = ag2_start(0, first)
    for c in sends:
        c.wait()
    finish_back(1, 0, chunks)

    sends = send_back(0)
    put_part(2, mm(dpre_t[...], all_of(h0)))
    own_back(0, h0)
    put_part(3, message_part(0, h0))
    second = rs1_start(1)
    first = ag1_start(0, first)
    second = rs2_start(1, second)
    second = ag2_start(1, second)
    for c in sends:
        c.wait()
    grad_stores = []
    for part_i in range(2):
        at = pl.ds(part_i * (rows // 2), rows // 2)
        finish_back(0, part_i * chunks // 2, (part_i + 1) * chunks // 2)
        c = pltpu.make_async_copy(g.at[at], grad_out.at[at], store_sem.at[1 + part_i])
        c.start()
        grad_stores.append(c)
    second = ag1_start(1, second)
    for c in first + second:
        c.wait()
    scale = 1.0 / (float(rows * ndp * nsec) ** 0.5)
    for m, out, layer in ((0, sg_out, 1), (1, mg_out, 1), (2, sg_out, 0), (3, mg_out, 0)):
        out[layer, :, :128] = g1[m, :width, :].astype(F32) * scale
        out[layer, :, 128:] = g1[m, width:, :].astype(F32) * scale
    hit_store.wait()
    for c in grad_stores:
        c.wait()


def finish_kernel(h_in, g_in, m_in, s_in, h_out, g_out, m_out, s_out, sems):
    copies = []
    for src, dst, pieces in ((g_in, g_out, 4), (h_in, h_out, 4), (m_in, m_out, 1), (s_in, s_out, 1)):
        size = src.shape[0] // pieces
        for p in range(pieces):
            at = pl.ds(p * size, size)
            c = pltpu.make_async_copy(src.at[at], dst.at[at], sems.at[len(copies)])
            c.start()
            copies.append(c)
    for c in copies:
        c.wait()


def per_device(ndp, nsec, hits, tiles, sources, send_list, w_message, w_self, cotangent):
    blocks, listed, tile = tiles.shape[1], tiles.shape[2], tiles.shape[3]
    rows, width = hits.shape[1], hits.shape[2]
    lent = send_list.shape[3]
    folded = 2 * width
    r1 = folded // ndp
    r2 = max(16, r1 // nsec)
    vmem, sem = pltpu.VMEM, pltpu.SemaphoreType.DMA
    scratch = [
        vmem((blocks, tile, width), BF), vmem((blocks, tile, width), BF), vmem((rows, width), BF),
        vmem((blocks * listed + 1, tile, tile), BF), vmem((rows, width), F32),
        vmem(w_message.shape, BF), vmem(w_self.shape, BF),
        vmem((blocks, tile, width), F32), vmem((blocks, tile, width), F32),
        vmem((rows, width), BF), vmem((2 * lent * tile, width), BF),
        vmem((rows, rows), BF), vmem((blocks, tile, 2 * lent * tile), BF),
        vmem((LAYERS, 2, lent * tile, width), BF), vmem((LAYERS, 2, lent * tile, width), BF),
        vmem((width, rows), F32), vmem((width, rows), F32),
        vmem((width, rows), BF), vmem((width, rows), BF), vmem((width, rows), F32),
        vmem((LAYERS, 2, lent, width, tile), BF),
        vmem((2, lent + 1, width, tile), BF), vmem((2, lent + 1, width, tile), BF),
        vmem((4, folded, 128), BF), vmem((ndp - 1, 4, r1, 128), BF), vmem((4, r1, 128), BF),
        vmem((nsec - 1, 4, r2, 128), BF), vmem((4, r2, 128), BF), vmem((4, r1, 128), BF),
        vmem((4, folded, 128), BF),
        sem((5,)), sem((3,)), sem((LAYERS, 2)), sem((LAYERS, 2)),
        sem((LAYERS, 2, lent // 2)), sem((LAYERS, 2, lent // 2)),
        sem((2, ndp - 1)), sem((2, ndp - 1)), sem((2, nsec - 1)), sem((2, nsec - 1)),
        sem((2, nsec - 1)), sem((2, nsec - 1)), sem((2, ndp - 1)), sem((2, ndp - 1)),
    ]
    flat = pl.BlockSpec(memory_space=pltpu.SMEM)
    far = pl.BlockSpec(memory_space=pl.ANY)
    near = pl.BlockSpec(memory_space=pltpu.VMEM)
    hit_output, grad, message_total, self_total = pl.pallas_call(
        functools.partial(kernel, ndp, nsec, blocks, listed, lent, tile, width, r1, r2),
        out_shape=(
            jax.ShapeDtypeStruct((rows, width), BF),
            jax.ShapeDtypeStruct((rows, width), F32),
            jax.ShapeDtypeStruct(w_message.shape, F32),
            jax.ShapeDtypeStruct(w_self.shape, F32),
        ),
        in_specs=[flat, flat, far, far, far, far, far],
        out_specs=(far, far, near, near),
        scratch_shapes=scratch,
        compiler_params=pltpu.CompilerParams(
            collective_id=0, has_side_effects=True, vmem_limit_bytes=56 * 1024 * 1024
        ),
    )(
        sources[0], send_list[0], hits[0].reshape(blocks, tile, width),
        tiles.reshape(blocks * listed, tile, tile), cotangent[0], w_message, w_self,
    )
    results = (hit_output, grad, message_total, self_total)
    hit_output, grad, message_total, self_total = pl.pallas_call(
        finish_kernel,
        out_shape=tuple(jax.ShapeDtypeStruct(x.shape, x.dtype) for x in results),
        in_specs=[far] * 4,
        out_specs=(far,) * 4,
        scratch_shapes=[sem((10,))],
    )(*results)
    return (hit_output[None], grad[None], message_total, self_total)


def solution(mesh):
    in_specs = (
        P("dp", "sector", None),
        P("dp", "sector", None, None, None),
        P("dp", "sector", None),
        P("dp", None, None, None),
        P(),
        P(),
        P("dp", "sector", None),
    )
    out_specs = (P("dp", "sector", None), P("dp", "sector", None), P(), P())
    return jax.shard_map(
        functools.partial(per_device, mesh.shape["dp"], mesh.shape["sector"]),
        mesh=mesh, in_specs=in_specs, out_specs=out_specs, check_vma=False,
    )
```

```python
import functools

import jax
import jax.numpy as jnp
from jax import lax
from jax.experimental import pallas as pl
from jax.experimental.pallas import tpu as pltpu
from jax.sharding import PartitionSpec as P

LAYERS = 2
CHUNK = 256
BF = jnp.bfloat16
F32 = jnp.float32
MESH = pl.DeviceIdType.MESH


def mm(a, b):
    return lax.dot_general(a, b, (((1,), (0,)), ((), ())), preferred_element_type=F32)


def silu_grad(pre):
    sig = jax.nn.sigmoid(pre)
    return sig * (1.0 + pre * (1.0 - sig))


def kernel(
    ndp, nsec, blocks, listed, lent, tile, width, r1, r2,
    src_ref, lists_ref, hits_hbm, tiles_hbm, cot_hbm, wm_hbm, ws_hbm,
    hit_out, grad_out, mg_out, sg_out,
    h0, h1, h2, tiles, g, wm_ref, ws_ref, pre0, pre1, msg, hmsg, a_own, a_halo, halo, lend,
    g_t, sg_t, dpre_t, dmsg_t, own_t, back_send, back_recv0, back_recv1,
    part, rs1, q1, rs2, r_own, g2, g1,
    load_sem, store_sem, halo_ss, halo_rs, back_ss, back_rs,
    rs1_ss, rs1_rs, rs2_ss, rs2_rs, ag2_ss, ag2_rs, ag1_ss, ag1_rs,
):
    back_recv = (back_recv0, back_recv1)
    rows = blocks * tile
    chunks = rows // CHUNK
    per_chunk = CHUNK // tile
    dp = lax.axis_index("dp")
    sec = lax.axis_index("sector")
    upper = lax.rem(sec + 1, nsec)
    lower = lax.rem(sec + nsec - 1, nsec)
    sec_peers = [lax.rem(sec + o, nsec) for o in range(1, nsec)]
    dp_peers = [lax.rem(dp + o, ndp) for o in range(1, ndp)]
    owners = r1 // r2

    loads = [
        pltpu.make_async_copy(hits_hbm, h0, load_sem.at[0]),
        pltpu.make_async_copy(wm_hbm, wm_ref, load_sem.at[1]),
        pltpu.make_async_copy(tiles_hbm, tiles.at[pl.ds(0, blocks * listed)], load_sem.at[2]),
        pltpu.make_async_copy(ws_hbm, ws_ref, load_sem.at[3]),
        pltpu.make_async_copy(cot_hbm, g, load_sem.at[4]),
    ]
    for c in loads:
        c.start()

    barrier = pltpu.get_barrier_semaphore()
    for p in sec_peers:
        pl.semaphore_signal(barrier, inc=1, device_id=(dp, p), device_id_type=MESH)
    for p in dp_peers:
        pl.semaphore_signal(barrier, inc=1, device_id=(p, sec), device_id_type=MESH)

    def cond(flag, fn):
        if owners == nsec:
            fn()
        else:
            pl.when(flag)(fn)

    def remote(src, dst, ss, rs, target):
        return pltpu.make_async_remote_copy(
            src_ref=src, dst_ref=dst, send_sem=ss, recv_sem=rs,
            device_id=target, device_id_type=MESH,
        )

    def block_rows(i):
        return pl.ds(pl.multiple_of(i * tile, tile), tile)

    def chunk_rows(i):
        return pl.ds(pl.multiple_of(i * CHUNK, CHUNK), CHUNK)

    def chunk_of(h, i):
        return h[pl.ds(i * per_chunk, per_chunk)].reshape(CHUNK, width)

    def all_of(h):
        return h[...].reshape(rows, width)

    def lent_block(d, i):
        return lists_ref[d, i, sec]

    def send_lent(layer, make):
        copies = []
        for d, target in ((0, upper), (1, lower)):
            if make is not None:
                lend[layer, d] = make([lent_block(d, i) for i in range(lent)])
            c = remote(
                lend.at[layer, d], halo.at[layer, d],
                halo_ss.at[layer, d], halo_rs.at[layer, d], (dp, target),
            )
            c.start()
            copies.append(c)
        return copies

    def own_messages(layer, h):
        @pl.loop(0, chunks)
        def _(i):
            msg[chunk_rows(i), :] = mm(chunk_of(h, i), wm_ref[layer]).astype(BF)

    def own_pre(layer, h, pre):
        @pl.loop(0, chunks)
        def _(i):
            r = chunk_rows(i)
            out = mm(a_own[r, :], msg[...]) + mm(chunk_of(h, i), ws_ref[layer])
            pre[pl.ds(i * per_chunk, per_chunk)] = out.reshape(per_chunk, tile, width)

    half = lent * tile

    def halo_messages(layer):
        for d in range(2):
            hmsg[d * half : (d + 1) * half, :] = mm(halo[layer, d], wm_ref[layer]).astype(BF)

    def halo_part(i):
        rows_a = a_halo[pl.ds(i * per_chunk, per_chunk)].reshape(CHUNK, 2 * half)
        return mm(rows_a, hmsg[...])

    def put_turned(dst, i, d):
        for j in range(per_chunk):
            at = pl.ds(pl.multiple_of(i * CHUNK + j * tile, tile), tile)
            dst[:, at] = d[j * tile : (j + 1) * tile, :].T

    loads[0].wait()
    for d in range(2):
        lend[0, d] = jnp.concatenate([h0[lent_block(d, i)] for i in range(lent)], axis=0)
    pl.semaphore_wait(barrier, nsec - 1 + ndp - 1)

    sends = send_lent(0, None)
    loads[1].wait()
    own_messages(0, h0)
    tiles[blocks * listed] = jnp.zeros((tile, tile), BF)
    back_recv0[:, lent] = jnp.zeros((2, width, tile), BF)
    back_recv1[:, lent] = jnp.zeros((2, width, tile), BF)
    loads[2].wait()

    slots = blocks + 2 * lent
    none = blocks * listed

    def least(pairs):
        best = jnp.int32(none)
        for index, away in pairs:
            best = jnp.minimum(best, index + none * (away * away))
        return best

    @pl.loop(0, blocks)
    def _(b):
        base = b * listed
        ids = [src_ref[k, b] for k in range(listed)]
        for k in reversed(range(listed - 1)):
            later = least([(base + m, ids[m] - ids[k]) for m in range(k + 1, listed)])
            tiles[base + k] = tiles[base + k] + tiles[later]
        for s in range(slots):
            val = tiles[least([(base + k, ids[k] - s) for k in range(listed)])]
            if s < blocks:
                a_own[block_rows(b), s * tile : (s + 1) * tile] = val
            else:
                o = s - blocks
                a_halo[b, :, o * tile : (o + 1) * tile] = val

    loads[3].wait()
    own_pre(0, h0, pre0)
    for c in sends:
        c.wait()
    halo_messages(0)

    def layer_out(h, pre):
        return (h.astype(F32) + pre * jax.nn.sigmoid(pre)).astype(BF)

    def lent_out(ids):
        pre = jnp.concatenate([pre0[b] for b in ids], axis=0)
        pre = pre + mm(jnp.concatenate([a_halo[b] for b in ids], axis=0), hmsg[...])
        return layer_out(jnp.concatenate([h0[b] for b in ids], axis=0), pre)

    sends = send_lent(1, lent_out)

    @pl.loop(0, chunks)
    def _(i):
        at = pl.ds(i * per_chunk, per_chunk)
        pre = chunk_of(pre0, i) + halo_part(i)
        h1[at] = layer_out(chunk_of(h0, i), pre).reshape(per_chunk, tile, width)
        pre0[at] = silu_grad(pre).reshape(per_chunk, tile, width)

    own_messages(1, h1)
    own_pre(1, h1, pre1)
    loads[4].wait()

    for c in sends:
        c.wait()
    halo_messages(1)

    @pl.loop(0, chunks, unroll=2)
    def _(i):
        r = chunk_rows(i)
        pre = chunk_of(pre1, i) + halo_part(i)
        sig = jax.nn.sigmoid(pre)
        h2[r, :] = (chunk_of(h1, i).astype(F32) + pre * sig).astype(BF)
        put_turned(dpre_t, i, (g[r, :] * (sig * (1.0 + pre * (1.0 - sig)))).astype(BF))

    hit_store = pltpu.make_async_copy(h2, hit_out, store_sem.at[0])
    hit_store.start()

    def send_back(layer):
        copies = []
        for d, target in ((0, lower), (1, upper)):
            for i in range(lent // 2):
                lo = (d * lent + 2 * i) * tile
                a_cols = a_halo[:, :, lo : lo + 2 * tile].reshape(rows, 2 * tile)
                res = mm(dpre_t[...], a_cols).astype(BF)
                back_send[layer, d, 2 * i] = res[:, :tile]
                back_send[layer, d, 2 * i + 1] = res[:, tile:]
                c = remote(
                    back_send.at[layer, d, pl.ds(2 * i, 2)], back_recv[layer].at[d, pl.ds(2 * i, 2)],
                    back_ss.at[layer, d, i], back_rs.at[layer, d, i], (dp, target),
                )
                c.start()
                copies.append(c)
        return copies

    def put_part(m, step_t):
        step = step_t.T.astype(BF)
        part[m, :width, :] = step[:, :128]
        part[m, width:, :] = step[:, 128:]

    def own_back(layer, h):
        @pl.loop(0, chunks)
        def _(i):
            out = mm(dpre_t[...], a_own[:, chunk_rows(i)])
            own_t[:, chunk_rows(i)] = out
            dmsg_t[:, chunk_rows(i)] = out.astype(BF)
            c = chunk_rows(i)
            g_t[:, c] = g_t[:, c] + mm(ws_ref[layer], dpre_t[:, c])

    def message_part(layer, h):
        total = mm(dmsg_t[...], all_of(h))
        for d in range(2):
            for i in range(lent):
                total = total + mm(back_send[layer, d, i], halo[layer, d, i * tile : (i + 1) * tile, :])
        return total

    def finish_back(layer, lo, hi):
        @pl.loop(lo, hi, unroll=2)
        def _(i):
            c = chunk_rows(i)
            lent_sum = []
            for j in range(per_chunk):
                b = i * per_chunk + j
                total = jnp.zeros((width, tile), F32)
                for d in range(2):
                    pos = jnp.int32(lent)
                    for k in range(lent):
                        away = lent_block(d, k) - b
                        pos = jnp.minimum(pos, k + lent * (away * away))
                    total = total + back_recv[layer][d, pos].astype(F32)
                lent_sum.append(total)
            total = (own_t[:, c] + jnp.concatenate(lent_sum, axis=1)).astype(BF)
            new = g_t[:, c] + mm(wm_ref[layer], total)
            if layer > 0:
                g_t[:, c] = new
                dpre_t[:, c] = (new * sg_t[:, c]).astype(BF)
            else:
                g[c, :] = new.T

    bounds = ((0, 2), (2, 2))

    def rs1_start(batch):
        m0, nb = bounds[batch]
        copies = []
        for o, p in enumerate(dp_peers):
            at = pl.ds(pl.multiple_of(p * r1, r1), r1)
            c = remote(
                part.at[pl.ds(m0, nb), at], rs1.at[o, pl.ds(m0, nb)],
                rs1_ss.at[batch, o], rs1_rs.at[batch, o], (p, sec),
            )
            c.start()
            copies.append(c)
        return copies

    def rs2_start(batch, copies):
        m0, nb = bounds[batch]
        for c in copies:
            c.wait()
        own = pl.ds(pl.multiple_of(dp * r1, r1), r1)
        for m in range(m0, m0 + nb):
            total = part[m, own, :].astype(F32)
            for o in range(ndp - 1):
                total = total + rs1[o, m].astype(F32)
            q1[m] = total.astype(BF)
        out = []
        for o, p in enumerate(sec_peers):
            piece = lax.rem(p, owners)
            at = pl.ds(pl.multiple_of(piece * r2, r2), r2)
            c = remote(
                q1.at[pl.ds(m0, nb), at], rs2.at[o, pl.ds(m0, nb)],
                rs2_ss.at[batch, o], rs2_rs.at[batch, o], (dp, p),
            )
            cond(p < owners, c.start)
            out.append((p, c))
        return out

    def ag2_start(batch, copies):
        m0, nb = bounds[batch]
        mine = lax.rem(sec, owners)
        at = pl.ds(pl.multiple_of(mine * r2, r2), r2)
        for p, c in copies:
            cond(p < owners, c.wait_send)
            cond(sec < owners, c.wait_recv)

        def total_up():
            for m in range(m0, m0 + nb):
                total = q1[m, at, :].astype(F32)
                for o in range(nsec - 1):
                    total = total + rs2[o, m].astype(F32)
                r_own[m] = total.astype(BF)
                g2[m, at, :] = r_own[m]

        cond(sec < owners, total_up)
        out = []
        for o, p in enumerate(sec_peers):
            c = remote(
                r_own.at[pl.ds(m0, nb)], g2.at[pl.ds(m0, nb), at],
                ag2_ss.at[batch, o], ag2_rs.at[batch, o], (dp, p),
            )
            cond(sec < owners, c.start)
            source = lax.rem(sec + nsec - 1 - o, nsec)
            out.append((source, c))
        return out

    def ag1_start(batch, copies):
        m0, nb = bounds[batch]
        for source, c in copies:
            cond(sec < owners, c.wait_send)
            cond(source < owners, c.wait_recv)
        at = pl.ds(pl.multiple_of(dp * r1, r1), r1)
        for m in range(m0, m0 + nb):
            g1[m, at, :] = g2[m]
        out = []
        for o, p in enumerate(dp_peers):
            c = remote(
                g2.at[pl.ds(m0, nb)], g1.at[pl.ds(m0, nb), at],
                ag1_ss.at[batch, o], ag1_rs.at[batch, o], (p, sec),
            )
            c.start()
            out.append(c)
        return out

    sends = send_back(1)

    @pl.loop(0, chunks)
    def _(i):
        put_turned(g_t, i, g[chunk_rows(i), :])
        put_turned(sg_t, i, chunk_of(pre0, i))

    put_part(0, mm(dpre_t[...], all_of(h1)))
    own_back(1, h1)
    put_part(1, message_part(1, h1))
    first = rs1_start(0)
    first = rs2_start(0, first)
    first = ag2_start(0, first)
    for c in sends:
        c.wait()
    finish_back(1, 0, chunks)

    sends = send_back(0)
    put_part(2, mm(dpre_t[...], all_of(h0)))
    own_back(0, h0)
    put_part(3, message_part(0, h0))
    second = rs1_start(1)
    first = ag1_start(0, first)
    second = rs2_start(1, second)
    second = ag2_start(1, second)
    for c in sends:
        c.wait()
    grad_stores = []
    for part_i in range(2):
        at = pl.ds(part_i * (rows // 2), rows // 2)
        finish_back(0, part_i * chunks // 2, (part_i + 1) * chunks // 2)
        c = pltpu.make_async_copy(g.at[at], grad_out.at[at], store_sem.at[1 + part_i])
        c.start()
        grad_stores.append(c)
    second = ag1_start(1, second)
    for c in first + second:
        c.wait()
    scale = 1.0 / (float(rows * ndp * nsec) ** 0.5)
    for m, out, layer in ((0, sg_out, 1), (1, mg_out, 1), (2, sg_out, 0), (3, mg_out, 0)):
        out[layer, :, :128] = g1[m, :width, :].astype(F32) * scale
        out[layer, :, 128:] = g1[m, width:, :].astype(F32) * scale
    hit_store.wait()
    for c in grad_stores:
        c.wait()


def finish_kernel(h_in, g_in, m_in, s_in, h_out, g_out, m_out, s_out):
    h_out[...] = h_in[...]
    g_out[...] = g_in[...]
    m_out[...] = m_in[...]
    s_out[...] = s_in[...]


def per_device(ndp, nsec, hits, tiles, sources, send_list, w_message, w_self, cotangent):
    blocks, listed, tile = tiles.shape[1], tiles.shape[2], tiles.shape[3]
    rows, width = hits.shape[1], hits.shape[2]
    lent = send_list.shape[3]
    folded = 2 * width
    r1 = folded // ndp
    r2 = max(16, r1 // nsec)
    vmem, sem = pltpu.VMEM, pltpu.SemaphoreType.DMA
    scratch = [
        vmem((blocks, tile, width), BF), vmem((blocks, tile, width), BF), vmem((rows, width), BF),
        vmem((blocks * listed + 1, tile, tile), BF), vmem((rows, width), F32),
        vmem(w_message.shape, BF), vmem(w_self.shape, BF),
        vmem((blocks, tile, width), F32), vmem((blocks, tile, width), F32),
        vmem((rows, width), BF), vmem((2 * lent * tile, width), BF),
        vmem((rows, rows), BF), vmem((blocks, tile, 2 * lent * tile), BF),
        vmem((LAYERS, 2, lent * tile, width), BF), vmem((LAYERS, 2, lent * tile, width), BF),
        vmem((width, rows), F32), vmem((width, rows), F32),
        vmem((width, rows), BF), vmem((width, rows), BF), vmem((width, rows), F32),
        vmem((LAYERS, 2, lent, width, tile), BF),
        vmem((2, lent + 1, width, tile), BF), vmem((2, lent + 1, width, tile), BF),
        vmem((4, folded, 128), BF), vmem((ndp - 1, 4, r1, 128), BF), vmem((4, r1, 128), BF),
        vmem((nsec - 1, 4, r2, 128), BF), vmem((4, r2, 128), BF), vmem((4, r1, 128), BF),
        vmem((4, folded, 128), BF),
        sem((5,)), sem((3,)), sem((LAYERS, 2)), sem((LAYERS, 2)),
        sem((LAYERS, 2, lent // 2)), sem((LAYERS, 2, lent // 2)),
        sem((2, ndp - 1)), sem((2, ndp - 1)), sem((2, nsec - 1)), sem((2, nsec - 1)),
        sem((2, nsec - 1)), sem((2, nsec - 1)), sem((2, ndp - 1)), sem((2, ndp - 1)),
    ]
    flat = pl.BlockSpec(memory_space=pltpu.SMEM)
    far = pl.BlockSpec(memory_space=pl.ANY)
    near = pl.BlockSpec(memory_space=pltpu.VMEM)
    hit_output, grad, message_total, self_total = pl.pallas_call(
        functools.partial(kernel, ndp, nsec, blocks, listed, lent, tile, width, r1, r2),
        out_shape=(
            jax.ShapeDtypeStruct((rows, width), BF),
            jax.ShapeDtypeStruct((rows, width), F32),
            jax.ShapeDtypeStruct(w_message.shape, F32),
            jax.ShapeDtypeStruct(w_self.shape, F32),
        ),
        in_specs=[flat, flat, far, far, far, far, far],
        out_specs=(far, far, near, near),
        scratch_shapes=scratch,
        compiler_params=pltpu.CompilerParams(
            collective_id=0, has_side_effects=True, vmem_limit_bytes=56 * 1024 * 1024
        ),
    )(
        sources[0].T, send_list[0].transpose(1, 2, 0), hits[0].reshape(blocks, tile, width),
        tiles.reshape(blocks * listed, tile, tile), cotangent[0], w_message, w_self,
    )
    wide = pl.BlockSpec((rows // 4, width), lambda i: (i, 0))
    deep = pl.BlockSpec((LAYERS, width // 4, width), lambda i: (0, i, 0))
    specs = [wide, wide, deep, deep]
    results = (hit_output, grad, message_total, self_total)
    hit_output, grad, message_total, self_total = pl.pallas_call(
        finish_kernel,
        out_shape=tuple(jax.ShapeDtypeStruct(x.shape, x.dtype) for x in results),
        grid=(4,),
        compiler_params=pltpu.CompilerParams(vmem_limit_bytes=56 * 1024 * 1024),
        in_specs=specs,
        out_specs=tuple(specs),
    )(*results)
    return (hit_output[None], grad[None], message_total, self_total)


def solution(mesh):
    in_specs = (
        P("dp", "sector", None),
        P("dp", "sector", None, None, None),
        P("dp", "sector", None),
        P("dp", None, None, None),
        P(),
        P(),
        P("dp", "sector", None),
    )
    out_specs = (P("dp", "sector", None), P("dp", "sector", None), P(), P())
    return jax.shard_map(
        functools.partial(per_device, mesh.shape["dp"], mesh.shape["sector"]),
        mesh=mesh, in_specs=in_specs, out_specs=out_specs, check_vma=False,
    )
```

```python
import functools

import jax
import jax.numpy as jnp
from jax import lax
from jax.experimental import pallas as pl
from jax.experimental.pallas import tpu as pltpu
from jax.sharding import PartitionSpec as P

LAYERS = 2
CHUNK = 256
BF = jnp.bfloat16
F32 = jnp.float32
MESH = pl.DeviceIdType.MESH


def mm(a, b):
    return lax.dot_general(a, b, (((1,), (0,)), ((), ())), preferred_element_type=F32)


def silu_grad(pre):
    sig = jax.nn.sigmoid(pre)
    return sig * (1.0 + pre * (1.0 - sig))


def kernel(
    ndp, nsec, blocks, listed, lent, tile, width, r1, r2,
    src_ref, lists_ref, hits_hbm, tiles_hbm, cot_hbm, wm_hbm, ws_hbm,
    hit_out, grad_out, last_out, sums_out,
    h0, h1, h2, tiles, g, wm_ref, ws_ref, pre0, pre1, msg, hmsg, a_own, a_halo, halo, lend,
    g_t, sg_t, dpre_t, dmsg_t, own_t, back_send, back_recv0, back_recv1,
    part, rs1, q1, rs2, r_own, g2, g1,
    load_sem, store_sem, halo_ss, halo_rs, back_ss, back_rs,
    rs1_ss, rs1_rs, rs2_ss, rs2_rs, ag2_ss, ag2_rs, ag1_ss, ag1_rs,
):
    back_recv = (back_recv0, back_recv1)
    rows = blocks * tile
    chunks = rows // CHUNK
    per_chunk = CHUNK // tile
    dp = lax.axis_index("dp")
    sec = lax.axis_index("sector")
    upper = lax.rem(sec + 1, nsec)
    lower = lax.rem(sec + nsec - 1, nsec)
    sec_peers = [lax.rem(sec + o, nsec) for o in range(1, nsec)]
    dp_peers = [lax.rem(dp + o, ndp) for o in range(1, ndp)]
    owners = r1 // r2

    loads = [
        pltpu.make_async_copy(hits_hbm, h0, load_sem.at[0]),
        pltpu.make_async_copy(wm_hbm, wm_ref, load_sem.at[1]),
        pltpu.make_async_copy(tiles_hbm, tiles.at[pl.ds(0, blocks * listed)], load_sem.at[2]),
        pltpu.make_async_copy(ws_hbm, ws_ref, load_sem.at[3]),
        pltpu.make_async_copy(cot_hbm, g, load_sem.at[4]),
    ]
    loads[0].start()

    barrier = pltpu.get_barrier_semaphore()
    for p in sec_peers:
        pl.semaphore_signal(barrier, inc=1, device_id=(dp, p), device_id_type=MESH)
    for p in dp_peers:
        pl.semaphore_signal(barrier, inc=1, device_id=(p, sec), device_id_type=MESH)

    def cond(flag, fn):
        if owners == nsec:
            fn()
        else:
            pl.when(flag)(fn)

    def remote(src, dst, ss, rs, target):
        return pltpu.make_async_remote_copy(
            src_ref=src, dst_ref=dst, send_sem=ss, recv_sem=rs,
            device_id=target, device_id_type=MESH,
        )

    def block_rows(i):
        return pl.ds(pl.multiple_of(i * tile, tile), tile)

    def chunk_rows(i):
        return pl.ds(pl.multiple_of(i * CHUNK, CHUNK), CHUNK)

    def chunk_of(h, i):
        return h[pl.ds(i * per_chunk, per_chunk)].reshape(CHUNK, width)

    def all_of(h):
        return h[...].reshape(rows, width)

    def lent_block(d, i):
        return lists_ref[d, i, sec]

    def send_lent(layer, make):
        copies = []
        for d, target in ((0, upper), (1, lower)):
            if make is not None:
                lend[layer, d] = make([lent_block(d, i) for i in range(lent)])
            c = remote(
                lend.at[layer, d], halo.at[layer, d],
                halo_ss.at[layer, d], halo_rs.at[layer, d], (dp, target),
            )
            c.start()
            copies.append(c)
        return copies

    def own_messages(layer, h):
        @pl.loop(0, chunks)
        def _(i):
            msg[chunk_rows(i), :] = mm(chunk_of(h, i), wm_ref[layer]).astype(BF)

    def own_pre(layer, h, pre):
        @pl.loop(0, chunks)
        def _(i):
            r = chunk_rows(i)
            out = mm(a_own[r, :], msg[...]) + mm(chunk_of(h, i), ws_ref[layer])
            pre[pl.ds(i * per_chunk, per_chunk)] = out.reshape(per_chunk, tile, width)

    half = lent * tile

    def halo_messages(layer):
        for d in range(2):
            hmsg[d * half : (d + 1) * half, :] = mm(halo[layer, d], wm_ref[layer]).astype(BF)

    def halo_part(i):
        rows_a = a_halo[pl.ds(i * per_chunk, per_chunk)].reshape(CHUNK, 2 * half)
        return mm(rows_a, hmsg[...])

    def put_turned(dst, i, d):
        for j in range(per_chunk):
            at = pl.ds(pl.multiple_of(i * CHUNK + j * tile, tile), tile)
            dst[:, at] = d[j * tile : (j + 1) * tile, :].T

    loads[0].wait()
    loads[1].start()
    loads[2].start()
    loads[3].start()
    for d in range(2):
        lend[0, d] = jnp.concatenate([h0[lent_block(d, i)] for i in range(lent)], axis=0)
    pl.semaphore_wait(barrier, nsec - 1 + ndp - 1)

    sends = send_lent(0, None)
    loads[1].wait()
    own_messages(0, h0)
    tiles[blocks * listed] = jnp.zeros((tile, tile), BF)
    back_recv0[:, lent] = jnp.zeros((2, width, tile), BF)
    back_recv1[:, lent] = jnp.zeros((2, width, tile), BF)
    loads[2].wait()

    slots = blocks + 2 * lent
    none = blocks * listed

    def least(pairs):
        best = jnp.int32(none)
        for index, away in pairs:
            best = jnp.minimum(best, index + none * (away * away))
        return best

    @pl.loop(0, blocks)
    def _(b):
        base = b * listed
        ids = [src_ref[k, b] for k in range(listed)]
        for k in reversed(range(listed - 1)):
            later = least([(base + m, ids[m] - ids[k]) for m in range(k + 1, listed)])
            tiles[base + k] = tiles[base + k] + tiles[later]
        for s in range(slots):
            val = tiles[least([(base + k, ids[k] - s) for k in range(listed)])]
            if s < blocks:
                a_own[block_rows(b), s * tile : (s + 1) * tile] = val
            else:
                o = s - blocks
                a_halo[b, :, o * tile : (o + 1) * tile] = val

    loads[3].wait()
    loads[4].start()
    own_pre(0, h0, pre0)
    for c in sends:
        c.wait()
    halo_messages(0)

    def layer_out(h, pre):
        return (h.astype(F32) + pre * jax.nn.sigmoid(pre)).astype(BF)

    def lent_out(ids):
        pre = jnp.concatenate([pre0[b] for b in ids], axis=0)
        pre = pre + mm(jnp.concatenate([a_halo[b] for b in ids], axis=0), hmsg[...])
        return layer_out(jnp.concatenate([h0[b] for b in ids], axis=0), pre)

    sends = send_lent(1, lent_out)

    @pl.loop(0, chunks)
    def _(i):
        at = pl.ds(i * per_chunk, per_chunk)
        pre = chunk_of(pre0, i) + halo_part(i)
        h1[at] = layer_out(chunk_of(h0, i), pre).reshape(per_chunk, tile, width)
        pre0[at] = silu_grad(pre).reshape(per_chunk, tile, width)

    own_messages(1, h1)
    own_pre(1, h1, pre1)
    loads[4].wait()

    for c in sends:
        c.wait()
    halo_messages(1)

    @pl.loop(0, chunks, unroll=2)
    def _(i):
        r = chunk_rows(i)
        pre = chunk_of(pre1, i) + halo_part(i)
        sig = jax.nn.sigmoid(pre)
        h2[r, :] = (chunk_of(h1, i).astype(F32) + pre * sig).astype(BF)
        put_turned(dpre_t, i, (g[r, :] * (sig * (1.0 + pre * (1.0 - sig)))).astype(BF))

    hit_store = pltpu.make_async_copy(h2, hit_out, store_sem.at[0])
    hit_store.start()

    def send_back(layer):
        copies = []
        for d, target in ((0, lower), (1, upper)):
            for i in range(lent // 2):
                lo = (d * lent + 2 * i) * tile
                a_cols = a_halo[:, :, lo : lo + 2 * tile].reshape(rows, 2 * tile)
                res = mm(dpre_t[...], a_cols).astype(BF)
                back_send[layer, d, 2 * i] = res[:, :tile]
                back_send[layer, d, 2 * i + 1] = res[:, tile:]
                c = remote(
                    back_send.at[layer, d, pl.ds(2 * i, 2)], back_recv[layer].at[d, pl.ds(2 * i, 2)],
                    back_ss.at[layer, d, i], back_rs.at[layer, d, i], (dp, target),
                )
                c.start()
                copies.append(c)
        return copies

    def put_part(m, step_t):
        step = step_t.T.astype(BF)
        part[m, :width, :] = step[:, :128]
        part[m, width:, :] = step[:, 128:]

    def own_back(layer, h):
        @pl.loop(0, chunks)
        def _(i):
            out = mm(dpre_t[...], a_own[:, chunk_rows(i)])
            own_t[:, chunk_rows(i)] = out
            dmsg_t[:, chunk_rows(i)] = out.astype(BF)
            c = chunk_rows(i)
            g_t[:, c] = g_t[:, c] + mm(ws_ref[layer], dpre_t[:, c])

    def message_part(layer, h):
        total = mm(dmsg_t[...], all_of(h))
        for d in range(2):
            for i in range(lent):
                total = total + mm(back_send[layer, d, i], halo[layer, d, i * tile : (i + 1) * tile, :])
        return total

    def finish_back(layer, lo, hi):
        @pl.loop(lo, hi, unroll=2)
        def _(i):
            c = chunk_rows(i)
            lent_sum = []
            for j in range(per_chunk):
                b = i * per_chunk + j
                total = jnp.zeros((width, tile), F32)
                for d in range(2):
                    pos = jnp.int32(lent)
                    for k in range(lent):
                        away = lent_block(d, k) - b
                        pos = jnp.minimum(pos, k + lent * (away * away))
                    total = total + back_recv[layer][d, pos].astype(F32)
                lent_sum.append(total)
            total = (own_t[:, c] + jnp.concatenate(lent_sum, axis=1)).astype(BF)
            if layer > 0:
                new = g_t[:, c] + mm(wm_ref[layer], total)
                g_t[:, c] = new
                dpre_t[:, c] = (new * sg_t[:, c]).astype(BF)
            else:
                dmsg_t[:, c] = total

    bounds = ((0, 2), (2, 2))

    def rs1_start(batch):
        m0, nb = bounds[batch]
        copies = []
        for o, p in enumerate(dp_peers):
            at = pl.ds(pl.multiple_of(p * r1, r1), r1)
            c = remote(
                part.at[pl.ds(m0, nb), at], rs1.at[o, pl.ds(m0, nb)],
                rs1_ss.at[batch, o], rs1_rs.at[batch, o], (p, sec),
            )
            c.start()
            copies.append(c)
        return copies

    def rs2_start(batch, copies):
        m0, nb = bounds[batch]
        for c in copies:
            c.wait()
        own = pl.ds(pl.multiple_of(dp * r1, r1), r1)
        for m in range(m0, m0 + nb):
            total = part[m, own, :].astype(F32)
            for o in range(ndp - 1):
                total = total + rs1[o, m].astype(F32)
            q1[m] = total.astype(BF)
        out = []
        for o, p in enumerate(sec_peers):
            piece = lax.rem(p, owners)
            at = pl.ds(pl.multiple_of(piece * r2, r2), r2)
            c = remote(
                q1.at[pl.ds(m0, nb), at], rs2.at[o, pl.ds(m0, nb)],
                rs2_ss.at[batch, o], rs2_rs.at[batch, o], (dp, p),
            )
            cond(p < owners, c.start)
            out.append((p, c))
        return out

    def ag2_start(batch, copies):
        m0, nb = bounds[batch]
        mine = lax.rem(sec, owners)
        at = pl.ds(pl.multiple_of(mine * r2, r2), r2)
        for p, c in copies:
            cond(p < owners, c.wait_send)
            cond(sec < owners, c.wait_recv)

        def total_up():
            for m in range(m0, m0 + nb):
                total = q1[m, at, :].astype(F32)
                for o in range(nsec - 1):
                    total = total + rs2[o, m].astype(F32)
                r_own[m] = total.astype(BF)
                g2[m, at, :] = r_own[m]

        cond(sec < owners, total_up)
        out = []
        for o, p in enumerate(sec_peers):
            c = remote(
                r_own.at[pl.ds(m0, nb)], g2.at[pl.ds(m0, nb), at],
                ag2_ss.at[batch, o], ag2_rs.at[batch, o], (dp, p),
            )
            cond(sec < owners, c.start)
            source = lax.rem(sec + nsec - 1 - o, nsec)
            out.append((source, c))
        return out

    def ag1_start(batch, copies):
        m0, nb = bounds[batch]
        for source, c in copies:
            cond(sec < owners, c.wait_send)
            cond(source < owners, c.wait_recv)
        at = pl.ds(pl.multiple_of(dp * r1, r1), r1)
        for m in range(m0, m0 + nb):
            g1[m, at, :] = g2[m]
        out = []
        for o, p in enumerate(dp_peers):
            c = remote(
                g2.at[pl.ds(m0, nb)], g1.at[pl.ds(m0, nb), at],
                ag1_ss.at[batch, o], ag1_rs.at[batch, o], (p, sec),
            )
            c.start()
            out.append(c)
        return out

    sends = send_back(1)

    @pl.loop(0, chunks)
    def _(i):
        put_turned(g_t, i, g[chunk_rows(i), :])
        put_turned(sg_t, i, chunk_of(pre0, i))

    put_part(0, mm(dpre_t[...], all_of(h1)))
    own_back(1, h1)
    put_part(1, message_part(1, h1))
    first = rs1_start(0)
    first = rs2_start(0, first)
    first = ag2_start(0, first)
    for c in sends:
        c.wait()
    finish_back(1, 0, chunks)

    sends = send_back(0)
    put_part(2, mm(dpre_t[...], all_of(h0)))
    own_back(0, h0)
    grad_store = pltpu.make_async_copy(g_t, grad_out, store_sem.at[1])
    grad_store.start()
    put_part(3, message_part(0, h0))
    second = rs1_start(1)
    first = ag1_start(0, first)
    second = rs2_start(1, second)
    second = ag2_start(1, second)
    for c in sends:
        c.wait()
    finish_back(0, 0, chunks)
    last_store = pltpu.make_async_copy(dmsg_t, last_out, store_sem.at[2])
    last_store.start()
    second = ag1_start(1, second)
    for c in first + second:
        c.wait()
    sums_store = pltpu.make_async_copy(g1, sums_out, store_sem.at[3])
    sums_store.start()
    for c in (hit_store, grad_store, last_store, sums_store):
        c.wait()


def finish_kernel(scale, h_in, g_in, last_in, sums_in, wm_ref, h_out, g_out, m_out, s_out):
    h_out[...] = h_in[...]
    g_out[...] = (g_in[...] + mm(wm_ref[0], last_in[...])).T
    for m, out, layer in ((0, s_out, 1), (1, m_out, 1), (2, s_out, 0), (3, m_out, 0)):
        out[layer, :, :128] = sums_in[m, 0].astype(F32) * scale
        out[layer, :, 128:] = sums_in[m, 1].astype(F32) * scale


def per_device(ndp, nsec, hits, tiles, sources, send_list, w_message, w_self, cotangent):
    blocks, listed, tile = tiles.shape[1], tiles.shape[2], tiles.shape[3]
    rows, width = hits.shape[1], hits.shape[2]
    lent = send_list.shape[3]
    folded = 2 * width
    r1 = folded // ndp
    r2 = max(16, r1 // nsec)
    vmem, sem = pltpu.VMEM, pltpu.SemaphoreType.DMA
    scratch = [
        vmem((blocks, tile, width), BF), vmem((blocks, tile, width), BF), vmem((rows, width), BF),
        vmem((blocks * listed + 1, tile, tile), BF), vmem((rows, width), F32),
        vmem(w_message.shape, BF), vmem(w_self.shape, BF),
        vmem((blocks, tile, width), F32), vmem((blocks, tile, width), F32),
        vmem((rows, width), BF), vmem((2 * lent * tile, width), BF),
        vmem((rows, rows), BF), vmem((blocks, tile, 2 * lent * tile), BF),
        vmem((LAYERS, 2, lent * tile, width), BF), vmem((LAYERS, 2, lent * tile, width), BF),
        vmem((width, rows), F32), vmem((width, rows), F32),
        vmem((width, rows), BF), vmem((width, rows), BF), vmem((width, rows), F32),
        vmem((LAYERS, 2, lent, width, tile), BF),
        vmem((2, lent + 1, width, tile), BF), vmem((2, lent + 1, width, tile), BF),
        vmem((4, folded, 128), BF), vmem((ndp - 1, 4, r1, 128), BF), vmem((4, r1, 128), BF),
        vmem((nsec - 1, 4, r2, 128), BF), vmem((4, r2, 128), BF), vmem((4, r1, 128), BF),
        vmem((4, folded, 128), BF),
        sem((5,)), sem((4,)), sem((LAYERS, 2)), sem((LAYERS, 2)),
        sem((LAYERS, 2, lent // 2)), sem((LAYERS, 2, lent // 2)),
        sem((2, ndp - 1)), sem((2, ndp - 1)), sem((2, nsec - 1)), sem((2, nsec - 1)),
        sem((2, nsec - 1)), sem((2, nsec - 1)), sem((2, ndp - 1)), sem((2, ndp - 1)),
    ]
    flat = pl.BlockSpec(memory_space=pltpu.SMEM)
    far = pl.BlockSpec(memory_space=pl.ANY)
    hit_rows, grad_t, last_t, sums = pl.pallas_call(
        functools.partial(kernel, ndp, nsec, blocks, listed, lent, tile, width, r1, r2),
        out_shape=(
            jax.ShapeDtypeStruct((rows, width), BF),
            jax.ShapeDtypeStruct((width, rows), F32),
            jax.ShapeDtypeStruct((width, rows), BF),
            jax.ShapeDtypeStruct((4, folded, 128), BF),
        ),
        in_specs=[flat, flat, far, far, far, far, far],
        out_specs=(far, far, far, far),
        scratch_shapes=scratch,
        compiler_params=pltpu.CompilerParams(
            collective_id=0, has_side_effects=True, vmem_limit_bytes=56 * 1024 * 1024
        ),
    )(
        sources[0].T, send_list[0].transpose(1, 2, 0), hits[0].reshape(blocks, tile, width),
        tiles.reshape(blocks * listed, tile, tile), cotangent[0], w_message, w_self,
    )
    steps = 4
    wide = pl.BlockSpec((rows // steps, width), lambda i: (i, 0))
    tall = pl.BlockSpec((width, rows // steps), lambda i: (0, i))
    deep = pl.BlockSpec((LAYERS, width // steps, width), lambda i: (0, i, 0))
    pair = pl.BlockSpec((4, 2, width // steps, 128), lambda i: (0, 0, i, 0))
    whole = pl.BlockSpec(w_message.shape, lambda i: (0, 0, 0))
    scale = 1.0 / (float(rows * ndp * nsec) ** 0.5)
    hit_output, grad, message_total, self_total = pl.pallas_call(
        functools.partial(finish_kernel, scale),
        out_shape=(
            jax.ShapeDtypeStruct((rows, width), BF),
            jax.ShapeDtypeStruct((rows, width), F32),
            jax.ShapeDtypeStruct(w_message.shape, F32),
            jax.ShapeDtypeStruct(w_self.shape, F32),
        ),
        grid=(steps,),
        compiler_params=pltpu.CompilerParams(vmem_limit_bytes=56 * 1024 * 1024),
        in_specs=[wide, tall, tall, pair, whole],
        out_specs=(wide, wide, deep, deep),
    )(hit_rows, grad_t, last_t, sums.reshape(4, 2, width, 128), w_message)
    return (hit_output[None], grad[None], message_total, self_total)


def solution(mesh):
    in_specs = (
        P("dp", "sector", None),
        P("dp", "sector", None, None, None),
        P("dp", "sector", None),
        P("dp", None, None, None),
        P(),
        P(),
        P("dp", "sector", None),
    )
    out_specs = (P("dp", "sector", None), P("dp", "sector", None), P(), P())
    return jax.shard_map(
        functools.partial(per_device, mesh.shape["dp"], mesh.shape["sector"]),
        mesh=mesh, in_specs=in_specs, out_specs=out_specs, check_vma=False,
    )
```
